32 devices in a mesh: lat: 2 (over x), lon: 16 (over z, y, core).
Axes of the slice: x: 2, y: 2, z: 4, core: 2. Of those that a mesh axis runs over, the one named last changes fastest.
Arguments:
- grid_state: bfloat16 [84, 32, 2048], P(None, 'lat', 'lon'), may hold values from -6 to 6
- mesh_feat: bfloat16 [8192, 1024], P(('lat', 'lon')), may hold values from -6 to 6
- enc_src: int32 [16, 8192], P(None, ('lat', 'lon')), may hold values from 0 to 5119, as said below
- enc_count: int32 [8192], P(('lat', 'lon')), may hold values from 1 to 16, as said below
- nbr_ids: int32 [32, 8192], P(None, ('lat', 'lon')), may hold values from 0 to 8191, as said below
- nbr_count: int32 [8192], P(('lat', 'lon')), may hold values from 2 to 32, as said below
- dec_src: int32 [3, 32, 2048], P(None, 'lat', 'lon'), may hold values from 0 to 8191, as said below
- w_embed: bfloat16 [84, 1024], replicated, may hold values from -0.625 to 0.625
- w_encode: bfloat16 [1024, 1024], replicated, may hold values from -0.1875 to 0.1875
- w_query: bfloat16 [1024, 1024], replicated, may hold values from -4 to 4
- w_key: bfloat16 [1024, 1024], replicated, may hold values from -4 to 4
- w_value: bfloat16 [1024, 1024], replicated, may hold values from -0.1875 to 0.1875
- w_output: bfloat16 [1024, 1024], replicated, may hold values from -0.1875 to 0.1875
- w_decode: bfloat16 [1024, 1024], replicated, may hold values from -0.1875 to 0.1875
- w_readout: bfloat16 [1024, 84], replicated, may hold values from -0.1875 to 0.1875
- norm_attn: float32 [1024], replicated, may hold values from 0.5 to 1.5
- norm_dec: float32 [1024], replicated, may hold values from 0.5 to 1.5
Outputs:
- denoised: float32 [84, 32, 2048], P(None, 'lat', 'lon')
The draws below stay inside these ranges and needn't reach their ends.
Inputs may be any that keep to these rules, and one draw needn't show every extreme that they name: `enc_src`: mesh node j belongs to block j // 256, numbered lat index times the number of lon indices plus lon index. Every entry of column j, padding included, names a cell of the window of 160 columns around that lon index's sector, in any row. `enc_count`: some node of every block has 16. `nbr_ids`: slot 0 of node j is j itself. The 32 slots of a node, padding included, are distinct mesh nodes whose block has the same or a cyclically adjacent lon index, and any lat index. `nbr_count`: some node of every block has 32. `dec_src`: the mesh nodes feeding cell (r, c) lie in blocks whose lon index is c // 128 or cyclically adjacent to it, any lat index.
All inputs are finite; a program needn't handle non-finite values.
Results may differ from the reference program's by a relative error of at most 0.0039.
Values may be sent and summed in bfloat16 or wider, within the bound.
No kernel may reach another device: no remote copies, remote signals or barrier semaphores. Data moves between devices by JAX's collectives and lax.ppermute only.
A program may use at most 128 MiB of HBM per device.

```python
import math
import jax
import jax.numpy as jnp
from jax import lax

V = 84
D = 1024
HEADS = 16
HEAD_DIM = 64
LAT_DEV = 16
LON_DEV = 128
HALO = 16
M_DEV = 256
KE = 16
KM = 32
LATS = 32
LONS = 2048
MESH = 8192
N_LAT = 2
N_LON = 16


def window_to_node(position, sector):
    band_index = position // (3 * M_DEV)
    offset = position // M_DEV % 3
    member = position % M_DEV
    return ((band_index * N_LON + (sector + offset - 1) % N_LON) * M_DEV + member).astype(jnp.int32)


def draw_enc_src(key, part):
    key = jax.random.fold_in(key, 101)
    node_total = M_DEV * N_LAT * N_LON
    row_key, col_key = jax.random.split(key)
    row_ids = jax.random.randint(row_key, (KE, node_total), 0, LAT_DEV * N_LAT)
    places = jax.random.randint(col_key, (KE, node_total), 0, LON_DEV + 2 * HALO)
    return (row_ids * (LON_DEV + 2 * HALO) + places).astype(jnp.int32)


def draw_enc_count(key, part):
    key = jax.random.fold_in(key, 102)
    node_total = M_DEV * N_LAT * N_LON
    counts = jax.random.randint(key, (node_total,), 1, KE + 1)
    return counts.at[::M_DEV].set(KE).astype(jnp.int32)


def draw_nbr_ids(key, part):
    key = jax.random.fold_in(key, 103)
    node_total = M_DEV * N_LAT * N_LON
    node_ids = jnp.arange(node_total, dtype=jnp.int32)
    device = node_ids // M_DEV
    band_index = device // N_LON
    sector = device % N_LON
    window = 3 * N_LAT * M_DEV
    stride = window // KM
    own_slot = (band_index * 3 + 1) * M_DEV + node_ids % M_DEV
    slot_index = jnp.arange(KM, dtype=jnp.int32)[:, None]
    jitter = jax.random.randint(key, (KM, node_total), 0, stride)
    offsets = jnp.where(slot_index == 0, 0, slot_index * stride + jitter)
    position = (own_slot[None, :] + offsets) % window
    return window_to_node(position, sector[None, :])


def draw_nbr_count(key, part):
    key = jax.random.fold_in(key, 104)
    node_total = M_DEV * N_LAT * N_LON
    counts = jax.random.randint(key, (node_total,), 2, KM + 1)
    return counts.at[::M_DEV].set(KM).astype(jnp.int32)


def draw_dec_src(key, part):
    key = jax.random.fold_in(key, 105)
    lat_total = LAT_DEV * N_LAT
    lon_total = LON_DEV * N_LON
    sector = (jnp.arange(lon_total, dtype=jnp.int32) // LON_DEV)[None, None, :]
    position = jax.random.randint(key, (3, lat_total, lon_total), 0, 3 * N_LAT * M_DEV)
    return window_to_node(position, sector)


def shared_projection(key, which):
    base_key = jax.random.fold_in(key, 107)
    own_part = jax.random.truncated_normal(jax.random.fold_in(base_key, which), -4.0, 4.0, (D, D), jnp.float32) / math.sqrt(D)
    return own_part


def draw_w_query(key, part):
    return shared_projection(key, 1).astype(jnp.bfloat16)


def draw_w_key(key, part):
    return shared_projection(key, 2).astype(jnp.bfloat16)


def level_of(stream_key, shape, cuts, smallest, largest):
    factor_of, own = 1.0, jax.random.fold_in(stream_key, 6)
    for dim, shards_of in cuts:
        draws = jnp.exp(jax.random.uniform(jax.random.fold_in(own, dim), (shards_of,), jnp.float32, smallest / len(cuts), largest / len(cuts)))
        factor_of = factor_of * jnp.repeat(draws, shape[dim] // shards_of).reshape([-1 if axis == dim else 1 for axis in range(len(shape))])
    return factor_of


def bell_draw(own_key, extent, deviation, reach, cuts=(), held_as=jnp.bfloat16):
    loudness = level_of(own_key, extent, cuts, -0.22, 0.18) if cuts else 1.0
    result = jax.random.normal(own_key, extent, jnp.float32) * deviation * loudness
    return jnp.minimum(jnp.maximum(result, -reach), reach).astype(held_as)


def setup_inputs(seed: int = 0) -> dict:
    splits = jax.random.split(jax.random.key(seed), 18)
    return {
        "grid_state": bell_draw(splits[0], (V, LATS, LONS), 1.0, 6.0, ((1, 2), (2, 16))),
        "mesh_feat": bell_draw(splits[1], (MESH, D), 1.0, 6.0, ((0, 32),)),
        "enc_src": draw_enc_src(jax.random.fold_in(splits[17], 71), 0),
        "enc_count": draw_enc_count(jax.random.fold_in(splits[17], 71), 0),
        "nbr_ids": draw_nbr_ids(jax.random.fold_in(splits[17], 71), 0),
        "nbr_count": draw_nbr_count(jax.random.fold_in(splits[17], 71), 0),
        "dec_src": draw_dec_src(jax.random.fold_in(splits[17], 71), 0),
        "w_embed": bell_draw(splits[7], (V, D), V ** -0.5, 0.625),
        "w_encode": bell_draw(splits[8], (D, D), D ** -0.5, 0.1875),
        "w_query": draw_w_query(jax.random.fold_in(splits[17], 71), 0),
        "w_key": draw_w_key(jax.random.fold_in(splits[17], 71), 0),
        "w_value": bell_draw(splits[11], (D, D), D ** -0.5, 0.1875),
        "w_output": bell_draw(splits[12], (D, D), D ** -0.5, 0.1875),
        "w_decode": bell_draw(splits[13], (D, D), D ** -0.5, 0.1875),
        "w_readout": bell_draw(splits[14], (D, V), D ** -0.5, 0.1875),
        "norm_attn": jnp.clip(1.0 + 0.1 * jax.random.normal(splits[15], (D,), jnp.float32), 0.5, 1.5),
        "norm_dec": jnp.clip(1.0 + 0.1 * jax.random.normal(splits[16], (D,), jnp.float32), 0.5, 1.5),
    }


def layer_norm(inputs_f, gain):
    centre = inputs_f - lax.optimization_barrier(jnp.mean(inputs_f, axis=-1, keepdims=True))
    spread = lax.optimization_barrier(jnp.mean(centre * centre, axis=-1, keepdims=True))
    return centre * lax.rsqrt(spread + 1e-05) * gain

def reference(grid_state, mesh_feat, enc_src, enc_count, nbr_ids, nbr_count, dec_src, w_embed, w_encode, w_query, w_key, w_value, w_output, w_decode, w_readout, norm_attn, norm_dec):
    lat_total = LAT_DEV * N_LAT
    lon_total = LON_DEV * N_LON
    block_count = N_LAT * N_LON
    node_total = M_DEV * block_count
    span_cols = LON_DEV + 2 * HALO
    flat_grid = grid_state.reshape(V, lat_total * lon_total)

    def encode_block(operands):
        source_block, count_block, block_id = operands
        sector = block_id % N_LON
        row_ids = source_block // span_cols
        col_ids = (sector * LON_DEV + source_block % span_cols - HALO) % lon_total
        cells = (row_ids * lon_total + col_ids).astype(jnp.int32)
        picked = jnp.take(flat_grid, cells, axis=1).astype(jnp.float32)
        live_slot = jnp.arange(KE, dtype=jnp.int32)[:, None] < count_block[None, :]
        summed = lax.optimization_barrier(jnp.sum(jnp.where(live_slot[None], picked, 0.0), axis=1))
        return summed / count_block.astype(jnp.float32)[None, :]
    sources = enc_src.reshape(KE, block_count, M_DEV).transpose(1, 0, 2)
    counts = enc_count.reshape(block_count, M_DEV)
    block_ids = jnp.arange(block_count, dtype=jnp.int32)
    mean_cells = lax.map(encode_block, (sources, counts, block_ids))
    mean_cells = mean_cells.transpose(1, 0, 2).reshape(V, node_total).astype(jnp.bfloat16)
    embedded = jax.nn.silu(jnp.dot(mean_cells.T, w_embed, preferred_element_type=jnp.float32)).astype(jnp.bfloat16)
    latent = mesh_feat.astype(jnp.float32) + jnp.dot(embedded, w_encode, preferred_element_type=jnp.float32)
    normed = layer_norm(latent, norm_attn).astype(jnp.bfloat16)
    queries = jnp.dot(normed, w_query, preferred_element_type=jnp.float32).astype(jnp.bfloat16)
    key_rows = jnp.dot(normed, w_key, preferred_element_type=jnp.float32).astype(jnp.bfloat16)
    value_rows = jnp.dot(normed, w_value, preferred_element_type=jnp.float32).astype(jnp.bfloat16)
    score_scale = HEAD_DIM ** (-0.5)

    def attend(operands):
        query_block, index_block, count_block = operands
        live_slot = jnp.arange(KM, dtype=jnp.int32)[:, None] < count_block[None, :]
        near_keys = jnp.take(key_rows, index_block, axis=0).astype(jnp.float32).reshape(KM, M_DEV, HEADS, HEAD_DIM)
        near_values = jnp.take(value_rows, index_block, axis=0).astype(jnp.float32).reshape(KM, M_DEV, HEADS, HEAD_DIM)
        query_heads = query_block.astype(jnp.float32).reshape(M_DEV, HEADS, HEAD_DIM)
        scores = jnp.einsum('bhd,kbhd->kbh', query_heads, near_keys) * score_scale
        scores = jnp.where(live_slot[:, :, None], scores, -jnp.inf)
        peak_score = lax.optimization_barrier(jnp.max(scores, axis=0, keepdims=True))
        expo_score = jnp.where(live_slot[:, :, None], jnp.exp(scores - peak_score), 0.0)
        weights = (expo_score / lax.optimization_barrier(jnp.sum(expo_score, axis=0, keepdims=True))).astype(jnp.bfloat16)
        context = jnp.einsum('kbh,kbhd->bhd', weights.astype(jnp.float32), near_values)
        return context.astype(jnp.bfloat16).reshape(M_DEV, D)
    query_blocks = queries.reshape(block_count, M_DEV, D)
    index_blocks = nbr_ids.reshape(KM, block_count, M_DEV).transpose(1, 0, 2)
    count_blocks = nbr_count.reshape(block_count, M_DEV)
    context = lax.map(attend, (query_blocks, index_blocks, count_blocks)).reshape(node_total, D)
    mixed = latent + jnp.dot(context, w_output, preferred_element_type=jnp.float32)
    normed_out = layer_norm(mixed, norm_dec).astype(jnp.bfloat16)
    decoded = jax.nn.silu(jnp.dot(normed_out, w_decode, preferred_element_type=jnp.float32)).astype(jnp.bfloat16)
    readout = jnp.dot(decoded, w_readout, preferred_element_type=jnp.float32).astype(jnp.bfloat16).T

    def decode_row(index_row):
        picked = jnp.take(readout, index_row, axis=1).astype(jnp.float32)
        return lax.optimization_barrier(jnp.sum(picked, axis=1)) / 3.0
    update = lax.map(decode_row, dec_src.transpose(1, 0, 2))
    return grid_state.astype(jnp.float32) + update.transpose(1, 0, 2)
```

```python
import functools

import jax
import jax.numpy as jnp
from jax import lax
from jax.experimental import pallas as pl
from jax.experimental.pallas import tpu as pltpu
from jax.sharding import PartitionSpec as P

HEADS = 16
HALO = 16
BF16 = jnp.bfloat16
F32 = jnp.float32
MIB = 1024 * 1024


def params(mib):
    return pltpu.CompilerParams(vmem_limit_bytes=mib * MIB)


def whole(memory=pltpu.VMEM):
    return pl.BlockSpec(memory_space=memory)


def silu(value):
    return 0.5 * value * (1.0 + jnp.tanh(0.5 * value))


def layer_norm(inputs_f, gain):
    centre = inputs_f - jnp.mean(inputs_f, axis=-1, keepdims=True)
    spread = jnp.mean(centre * centre, axis=-1, keepdims=True)
    return centre * lax.rsqrt(spread + 1e-05) * gain


def from_bands(value):
    count = lax.axis_size("lat")
    return [
        lax.ppermute(value, "lat", [(i, (i - step) % count) for i in range(count)])
        for step in range(1, count)
    ]


def from_sides(value):
    count = lax.axis_size("lon")
    west = lax.ppermute(value, "lon", [(i, (i + 1) % count) for i in range(count)])
    east = lax.ppermute(value, "lon", [(i, (i - 1) % count) for i in range(count)])
    return west, east


def quotient(value_f, divisor):
    return jnp.floor((value_f + 0.5) * (1.0 / divisor))


def prep_kernel(grid_ref, src_ref, count_ref, flat_ref, low_ref, high_ref, live_ref, wide):
    rows, cols = grid_ref.shape[1:]
    wide[...] = grid_ref[...].astype(F32)
    for row in range(rows):
        line = wide[:, row, :]
        flat_ref[:, row * cols : (row + 1) * cols] = line.astype(BF16)
        low_ref[:, row * HALO : (row + 1) * HALO] = line[:, :HALO].astype(BF16)
        high_ref[:, row * HALO : (row + 1) * HALO] = line[:, cols - HALO :].astype(BF16)
    slot = lax.broadcasted_iota(jnp.int32, src_ref.shape, 0)
    live_ref[...] = jnp.where(slot < count_ref[...], src_ref[...], -1)


def encode_kernel(place_ref, src_ref, flat_ref, west_ref, east_ref, out_ref, counts):
    slots, nodes = src_ref.shape
    cells = flat_ref.shape[1]
    rows = west_ref.shape[1] // HALO
    cols = cells // rows
    span = cols + 2 * HALO
    lanes = 128
    source = src_ref[...].astype(F32)
    row_of = quotient(source, span)
    col_of = source - row_of * span
    row_of = row_of - (place_ref[0] * rows).astype(F32)
    iota = lax.broadcasted_iota(jnp.int32, (span, lanes), 0).astype(F32).astype(BF16)
    one = jnp.ones((span, lanes), BF16)
    none = jnp.zeros((span, lanes), BF16)
    for row in range(rows):
        code = jnp.where(row_of == row, col_of, -1.0).astype(BF16)
        for tile in range(nodes // lanes):
            at = slice(tile * lanes, (tile + 1) * lanes)
            total = none
            for slot in range(slots):
                total = total + jnp.where(iota == code[slot : slot + 1, at], one, none)
            counts[row * cols : (row + 1) * cols, at] = total[HALO : HALO + cols]
            counts[cells + row * HALO : cells + (row + 1) * HALO, at] = total[:HALO]
            counts[cells + (rows + row) * HALO : cells + (rows + row + 1) * HALO, at] = total[
                HALO + cols :
            ]
    rim = rows * HALO
    summed = jnp.dot(flat_ref[...], counts[:cells], preferred_element_type=F32)
    summed += jnp.dot(west_ref[...], counts[cells : cells + rim], preferred_element_type=F32)
    summed += jnp.dot(east_ref[...], counts[cells + rim :], preferred_element_type=F32)
    out_ref[...] = summed


def mean_kernel(src_ref, own_ref, *refs):
    others, out_ref = refs[:-1], refs[-1]
    bands = len(others) + 1
    nodes = own_ref.shape[1] // bands
    count = jnp.sum(jnp.where(src_ref[...] >= 0, 1.0, 0.0), axis=0, keepdims=True)
    for band in range(bands):
        at = slice(band * nodes, (band + 1) * nodes)
        total = own_ref[:, at]
        for step, other in enumerate(others, 1):
            there = (band - step) % bands
            total = total + other[:, there * nodes : (there + 1) * nodes]
        out_ref[:, at] = (total / count[:, at]).astype(BF16)


def place_of(ids, place_ref, node_count, bands, sectors):
    ids_f = ids.astype(F32)
    device = quotient(ids_f, node_count)
    member = ids_f - device * node_count
    band = quotient(device, sectors)
    away = device - band * sectors - place_ref[1].astype(F32)
    side = jnp.where(away == 0, 0.0, 2.0)
    side = jnp.where((away == -1) | (away == sectors - 1), 1.0, side)
    band = band - place_ref[0].astype(F32)
    band = jnp.where(band < 0, band + bands, band)
    return side * bands + band, member


def bias_kernel(bands, sectors, place_ref, ids_ref, count_ref, out_ref):
    slots, nodes = ids_ref.shape
    lanes = 128
    block, member = place_of(ids_ref[...], place_ref, nodes, bands, sectors)
    slot_of = lax.broadcasted_iota(jnp.int32, (slots, nodes), 0)
    block = jnp.where(slot_of < count_ref[...], block, -1.0)
    iota = lax.broadcasted_iota(jnp.int32, (nodes, lanes), 0).astype(F32).astype(BF16)
    shut = jnp.full((nodes, lanes), -1e30, BF16)
    opened = jnp.zeros((nodes, lanes), BF16)
    for part in range(3 * bands):
        code = jnp.where(block == part, member, -1.0).astype(BF16)
        for tile in range(nodes // lanes):
            at = slice(tile * lanes, (tile + 1) * lanes)
            total = shut
            for slot in range(slots):
                total = jnp.where(iota == code[slot : slot + 1, at], opened, total)
            out_ref[at, part * nodes : (part + 1) * nodes] = total.astype(F32).T


def latent_of(mean, feat, w_embed, w_encode):
    embedded = silu(
        lax.dot_general(mean, w_embed, (((0,), (0,)), ((), ())), preferred_element_type=F32)
    ).astype(BF16)
    return feat.astype(F32) + jnp.dot(embedded, w_encode, preferred_element_type=F32)


def sector_kernel(
    mean_ref, feat_ref, gain_ref, w_embed, w_encode, w_query, w_key, w_value,
    latent_ref, query_ref, key_ref, value_ref,
):
    nodes = latent_ref.shape[0]
    for part in range(feat_ref.shape[0] // nodes):
        at = slice(part * nodes, (part + 1) * nodes)
        latent = latent_of(mean_ref[:, at], feat_ref[at], w_embed[...], w_encode[...])
        normed = layer_norm(latent, gain_ref[...]).astype(BF16)
        if part == 0:
            latent_ref[...] = latent
            query_ref[...] = jnp.dot(normed, w_query[...], preferred_element_type=F32).astype(BF16)
        key_ref[at] = jnp.dot(normed, w_key[...], preferred_element_type=F32).astype(BF16)
        value_ref[at] = jnp.dot(normed, w_value[...], preferred_element_type=F32).astype(BF16)


def attend_kernel(
    mean_w, mean_e, feat_w, feat_e, bias_ref, latent_ref, query_ref, key_own, value_own,
    gain_ref, gain_dec_ref, w_embed, w_encode, w_key, w_value, w_output, w_decode, w_read,
    out_ref, key_ref, value_ref, score_ref, weight_ref, context_ref,
):
    nodes, features = latent_ref.shape
    sector_nodes = feat_w.shape[0]
    key_ref[:sector_nodes] = key_own[...]
    value_ref[:sector_nodes] = value_own[...]
    for side, (mean_ref, feat_ref) in enumerate(((mean_w, feat_w), (mean_e, feat_e)), 1):
        for part in range(sector_nodes // nodes):
            at = slice(part * nodes, (part + 1) * nodes)
            to = slice(side * sector_nodes + part * nodes, side * sector_nodes + (part + 1) * nodes)
            latent = latent_of(mean_ref[:, at], feat_ref[at], w_embed[...], w_encode[...])
            normed = layer_norm(latent, gain_ref[...]).astype(BF16)
            key_ref[to] = jnp.dot(normed, w_key[...], preferred_element_type=F32).astype(BF16)
            value_ref[to] = jnp.dot(normed, w_value[...], preferred_element_type=F32).astype(BF16)

    width = features // HEADS
    group = 256
    per_group = group // width
    scale = width**-0.5
    chunk = 16
    head_of = lax.broadcasted_iota(jnp.int32, (nodes, group), 1) // width

    def attend(step, carry):
        at = pl.ds(pl.multiple_of(step * group, group), group)
        query = (query_ref[:, at].astype(F32) * scale)
        keys = key_ref[:, at]
        values = value_ref[:, at]
        gathered = jnp.zeros((nodes, group), F32)
        for head in range(per_group):
            own = jnp.where(head_of == head, query, 0.0).astype(BF16)
            score_ref[head] = lax.dot_general(
                own, keys, (((1,), (1,)), ((), ())), preferred_element_type=F32
            )
            sums = []
            for start in range(0, nodes, chunk):
                rows = slice(start, start + chunk)
                scores = score_ref[head, rows] + bias_ref[rows]
                peak = jnp.max(scores, axis=1, keepdims=True)
                expo = jnp.exp(scores - peak)
                sums.append(jnp.sum(expo, axis=1, keepdims=True))
                weight_ref[head, rows] = expo.astype(BF16)
            total = jnp.concatenate(sums, axis=0)
            mixed = jnp.dot(weight_ref[head], values, preferred_element_type=F32)
            gathered = jnp.where(head_of == head, mixed / total, gathered)
        context_ref[:, at] = gathered.astype(BF16)
        return carry

    lax.fori_loop(0, features // group, attend, 0)
    mixed = latent_ref[...] + jnp.dot(context_ref[...], w_output[...], preferred_element_type=F32)
    normed_out = layer_norm(mixed, gain_dec_ref[...]).astype(BF16)
    decoded = silu(jnp.dot(normed_out, w_decode[...], preferred_element_type=F32)).astype(BF16)
    out_ref[...] = lax.dot_general(
        w_read[...], decoded, (((0,), (1,)), ((), ())), preferred_element_type=F32
    ).astype(BF16)


def decode_kernel(bands, sectors, nodes, place_ref, dec_ref, own_ref, west_ref, east_ref, grid_ref, out_ref):
    rows, cols = grid_ref.shape[1:]
    iota = lax.broadcasted_iota(jnp.int32, (nodes, cols), 0).astype(F32).astype(BF16)
    one = jnp.ones((nodes, cols), BF16)
    none = jnp.zeros((nodes, cols), BF16)
    block, member = place_of(dec_ref[...], place_ref, nodes, bands, sectors)
    for row in range(rows):
        update = jnp.zeros((grid_ref.shape[0], cols), F32)
        for part in range(3 * bands):
            code = jnp.where(block[:, row] == part, member[:, row], -1.0).astype(BF16)
            counts = none
            for slot in range(code.shape[0]):
                counts = counts + jnp.where(iota == code[slot : slot + 1], one, none)
            side, band = divmod(part, bands)
            ref = (own_ref, west_ref, east_ref)[side]
            update += jnp.dot(
                ref[:, band * nodes : (band + 1) * nodes], counts, preferred_element_type=F32
            )
        out_ref[:, row, :] = update / 3.0
    out_ref[...] += grid_ref[...].astype(F32)


def call(kernel, outs, operands, scratch=(), scalars=0, mib=48, flops=0, moved=0):
    specs = [whole(pltpu.SMEM)] * scalars + [whole()] * (len(operands) - scalars)
    single = not isinstance(outs, (list, tuple))
    return pl.pallas_call(
        kernel,
        out_shape=outs,
        in_specs=specs,
        out_specs=whole() if single else [whole()] * len(outs),
        scratch_shapes=list(scratch),
        compiler_params=params(mib),
        cost_estimate=pl.CostEstimate(flops=flops, bytes_accessed=moved, transcendentals=0),
    )(*operands)


def body(
    grid_state, mesh_feat, enc_src, enc_count, nbr_ids, nbr_count, dec_src,
    w_embed, w_encode, w_query, w_key, w_value, w_output, w_decode, w_readout, norm_attn, norm_dec,
):
    shape = jax.ShapeDtypeStruct
    bands, sectors = lax.axis_size("lat"), lax.axis_size("lon")
    place = jnp.stack([lax.axis_index("lat"), lax.axis_index("lon")]).astype(jnp.int32)
    variables, rows, cols = grid_state.shape
    nodes, features = mesh_feat.shape
    slots = enc_src.shape[0]
    cells, rim = rows * cols, rows * HALO
    sector_nodes = bands * nodes
    window = 3 * sector_nodes

    flat, low, high, live = call(
        prep_kernel,
        [
            shape((variables, cells), BF16),
            shape((variables, rim), BF16),
            shape((variables, rim), BF16),
            shape((slots, nodes), jnp.int32),
        ],
        (grid_state, enc_src, enc_count[None]),
        [pltpu.VMEM((variables, rows, cols), F32)],
    )
    sources = jnp.concatenate([live] + from_bands(live), axis=1)
    west_rim = from_sides(high)[0]
    east_rim = from_sides(low)[1]
    feats = jnp.concatenate([mesh_feat] + from_bands(mesh_feat), axis=0)
    feat_w, feat_e = from_sides(feats)
    bias = call(
        functools.partial(bias_kernel, bands, sectors),
        shape((nodes, window), F32),
        (place, nbr_ids, nbr_count[None]),
        scalars=1,
        flops=10_000_000,
        moved=8_000_000,
    )
    summed = call(
        encode_kernel,
        shape((variables, sector_nodes), F32),
        (place, sources, flat, west_rim, east_rim),
        [pltpu.VMEM((cells + 2 * rim, sector_nodes), BF16)],
        scalars=1,
    )
    mean = call(
        mean_kernel,
        shape((variables, sector_nodes), BF16),
        (sources, summed, *from_bands(summed)),
    )
    mean_w, mean_e = from_sides(mean)
    gain = norm_attn[None]
    latent, query, key, value = call(
        sector_kernel,
        [
            shape((nodes, features), F32),
            shape((nodes, features), BF16),
            shape((sector_nodes, features), BF16),
            shape((sector_nodes, features), BF16),
        ],
        (mean, feats, gain, w_embed, w_encode, w_query, w_key, w_value),
        flops=4_000_000_000,
        moved=12_000_000,
    )
    per_group = 256 * HEADS // features
    readout = call(
        attend_kernel,
        shape((variables, nodes), BF16),
        (
            mean_w, mean_e, feat_w, feat_e, bias, latent, query, key, value,
            gain, norm_dec[None], w_embed, w_encode, w_key, w_value, w_output, w_decode, w_readout,
        ),
        [
            pltpu.VMEM((window, features), BF16),
            pltpu.VMEM((window, features), BF16),
            pltpu.VMEM((per_group, nodes, window), F32),
            pltpu.VMEM((per_group, nodes, window), BF16),
            pltpu.VMEM((nodes, features), BF16),
        ],
        mib=60,
    )
    reads = jnp.concatenate([readout] + from_bands(readout), axis=1)
    read_w, read_e = from_sides(reads)
    return call(
        functools.partial(decode_kernel, bands, sectors, nodes),
        shape(grid_state.shape, F32),
        (place, dec_src, reads, read_w, read_e, grid_state),
        scalars=1,
    )


def solution(mesh):
    in_specs = (
        P(None, "lat", "lon"),
        P(("lat", "lon"), None),
        P(None, ("lat", "lon")),
        P(("lat", "lon")),
        P(None, ("lat", "lon")),
        P(("lat", "lon")),
        P(None, "lat", "lon"),
    ) + (P(),) * 10
    out_specs = P(None, "lat", "lon")
    return jax.shard_map(body, mesh=mesh, in_specs=in_specs, out_specs=out_specs, check_vma=False)
```

```python
import functools

import jax
import jax.numpy as jnp
from jax import lax
from jax.experimental import pallas as pl
from jax.experimental.pallas import tpu as pltpu
from jax.sharding import PartitionSpec as P

HEADS = 16
HALO = 16
BF16 = jnp.bfloat16
F32 = jnp.float32
MIB = 1024 * 1024


def params(mib):
    return pltpu.CompilerParams(vmem_limit_bytes=mib * MIB)


def whole(memory=pltpu.VMEM):
    return pl.BlockSpec(memory_space=memory)


def silu(value):
    return 0.5 * value * (1.0 + jnp.tanh(0.5 * value))


def layer_norm(inputs_f, gain):
    centre = inputs_f - jnp.mean(inputs_f, axis=-1, keepdims=True)
    spread = jnp.mean(centre * centre, axis=-1, keepdims=True)
    return centre * lax.rsqrt(spread + 1e-05) * gain


def from_bands(value):
    count = lax.axis_size("lat")
    return [
        lax.ppermute(value, "lat", [(i, (i - step) % count) for i in range(count)])
        for step in range(1, count)
    ]


def from_near(value):
    count = lax.axis_size("lon")
    return lax.ppermute(value, "lon", [(i, i ^ 1) for i in range(count)])


def from_far(value):
    count = lax.axis_size("lon")
    return lax.ppermute(value, "lon", [(i, (i - 1 + 2 * (i % 2)) % count) for i in range(count)])


def quotient(value_f, divisor):
    return jnp.floor((value_f + 0.5) * (1.0 / divisor))


def prep_kernel(place_ref, grid, src, count, flat_ref, near_ref, far_ref, live_ref, wide):
    slot = lax.broadcasted_iota(jnp.int32, live_ref.shape, 0)
    live_ref[...] = jnp.where(slot < count.now()[...], src.now()[...], -1)
    grid_ref = grid.now()
    rows, cols = grid_ref.shape[1:]
    per_tile = cols // HALO
    odd = place_ref[1] % 2
    near_at = jnp.where(odd == 0, cols - HALO, 0)
    far_at = cols - HALO - near_at
    lane = lax.broadcasted_iota(jnp.int32, (grid_ref.shape[0], cols), 1) // HALO
    wide[...] = grid_ref[...].astype(F32)
    for tile in range(rows // per_tile):
        near, far = None, None
        for place in range(per_tile):
            row = tile * per_tile + place
            line = wide[:, row, :]
            flat_ref[:, row * cols : (row + 1) * cols] = line.astype(BF16)
            turned = [
                pltpu.roll(line, (place * HALO - start + cols) % cols, 1)
                for start in (near_at, far_at)
            ]
            near = turned[0] if near is None else jnp.where(lane == place, turned[0], near)
            far = turned[1] if far is None else jnp.where(lane == place, turned[1], far)
        near_ref[:, tile * cols : (tile + 1) * cols] = near.astype(BF16)
        far_ref[:, tile * cols : (tile + 1) * cols] = far.astype(BF16)


def encode_kernel(place_ref, src_ref, flat_ref, out_ref, rim_ref, counts):
    slots, nodes = src_ref.shape
    cells = flat_ref.shape[1]
    rim = rim_ref.shape[0] // 2
    rows = rim // HALO
    cols = cells // rows
    span = cols + 2 * HALO
    lanes = 128
    even = place_ref[1] % 2 == 0
    source = src_ref[...].astype(F32)
    row_of = quotient(source, span)
    col_of = source - row_of * span
    row_of = row_of - (place_ref[0] * rows).astype(F32)
    iota = lax.broadcasted_iota(jnp.int32, (span, lanes), 0).astype(F32).astype(BF16)
    one = jnp.ones((span, lanes), BF16)
    none = jnp.zeros((span, lanes), BF16)
    west = pl.multiple_of(jnp.where(even, rim, 0), rim)
    east = pl.multiple_of(jnp.where(even, 0, rim), rim)
    for row in range(rows):
        code = jnp.where(row_of == row, col_of, -1.0).astype(BF16)
        for tile in range(nodes // lanes):
            at = slice(tile * lanes, (tile + 1) * lanes)
            total = none
            for slot in range(slots):
                total = total + jnp.where(iota == code[slot : slot + 1, at], one, none)
            counts[row * cols : (row + 1) * cols, at] = total[HALO : HALO + cols]
            rim_ref[pl.ds(west + row * HALO, HALO), at] = total[:HALO]
            rim_ref[pl.ds(east + row * HALO, HALO), at] = total[HALO + cols :]
    out_ref[...] = jnp.dot(flat_ref[...], counts[...], preferred_element_type=F32)


def rim_kernel(near_ref, far_ref, *refs):
    out_ref = refs[-1]
    rim = near_ref.shape[1]
    for part in range(len(refs) // 2):
        summed, counts = refs[2 * part], refs[2 * part + 1]
        nodes = summed.shape[1]
        total = summed[...]
        total += jnp.dot(near_ref[...], counts[:rim], preferred_element_type=F32)
        total += jnp.dot(far_ref[...], counts[rim:], preferred_element_type=F32)
        out_ref[:, part * nodes : (part + 1) * nodes] = total


def mean_kernel(own_ref, *refs):
    out_ref = refs[-1]
    bands = len(refs) // 2
    others, sources = refs[: bands - 1], refs[bands - 1 : -1]
    nodes = own_ref.shape[1] // bands
    for band in range(bands):
        at = slice(band * nodes, (band + 1) * nodes)
        count = jnp.sum(jnp.where(sources[band][...] >= 0, 1.0, 0.0), axis=0, keepdims=True)
        total = own_ref[:, at]
        for step, other in enumerate(others, 1):
            there = (band - step) % bands
            total = total + other[:, there * nodes : (there + 1) * nodes]
        out_ref[:, at] = (total / count).astype(BF16)


def place_of(ids, place_ref, node_count, bands, sectors):
    ids_f = ids.astype(F32)
    device = quotient(ids_f, node_count)
    member = ids_f - device * node_count
    band = quotient(device, sectors)
    sector = device - band * sectors
    mine = place_ref[1]
    near = mine + 1 - 2 * (mine % 2)
    side = jnp.where(sector == mine.astype(F32), 0.0, 2.0)
    side = jnp.where(sector == near.astype(F32), 1.0, side)
    band = band - place_ref[0].astype(F32)
    band = jnp.where(band < 0, band + bands, band)
    return side * bands + band, member


def bias_kernel(bands, sectors, place_ref, ids, count, own_ref, rest_ref):
    ids_ref, count_ref = ids.now(), count.now()
    slots, nodes = ids_ref.shape
    lanes = 128
    block, member = place_of(ids_ref[...], place_ref, nodes, bands, sectors)
    slot_of = lax.broadcasted_iota(jnp.int32, (slots, nodes), 0)
    block = jnp.where(slot_of < count_ref[...], block, -1.0)
    iota = lax.broadcasted_iota(jnp.int32, (nodes, lanes), 0).astype(F32).astype(BF16)
    shut = jnp.full((nodes, lanes), -1e30, BF16)
    opened = jnp.zeros((nodes, lanes), BF16)
    for part in range(3 * bands):
        code = jnp.where(block == part, member, -1.0).astype(BF16)
        ref, index = (own_ref, part) if part < bands else (rest_ref, part - bands)
        for tile in range(nodes // lanes):
            at = slice(tile * lanes, (tile + 1) * lanes)
            total = shut
            for slot in range(slots):
                total = jnp.where(iota == code[slot : slot + 1, at], opened, total)
            ref[at, index * nodes : (index + 1) * nodes] = total.astype(F32).T


def latent_of(mean, feat, w_embed, w_encode):
    embedded = silu(
        lax.dot_general(mean, w_embed, (((0,), (0,)), ((), ())), preferred_element_type=F32)
    ).astype(BF16)
    return feat.astype(F32) + jnp.dot(embedded, w_encode, preferred_element_type=F32)


def sector_rows(
    mean_ref, gain_ref, w_embed, w_encode, w_query, w_key, w_value, feats, latent_ref, query_ref, pair_ref
):
    nodes, features = feats[0].shape
    for part, feat in enumerate(feats):
        at = slice(part * nodes, (part + 1) * nodes)
        latent = latent_of(mean_ref[:, at], feat[...], w_embed[...], w_encode[...])
        normed = layer_norm(latent, gain_ref[...]).astype(BF16)
        if part == 0 and latent_ref is not None:
            latent_ref[...] = latent
            query_ref[...] = jnp.dot(normed, w_query[...], preferred_element_type=F32).astype(BF16)
        pair_ref[at, :features] = jnp.dot(
            normed, w_key[...], preferred_element_type=F32
        ).astype(BF16)
        pair_ref[at, features:] = jnp.dot(
            normed, w_value[...], preferred_element_type=F32
        ).astype(BF16)


LANES = 128
CHUNK = 16


def head_scores(query_ref, pairs, at, head, score_ref):
    nodes = query_ref.shape[0]
    width = LANES // 2
    lane = lax.broadcasted_iota(jnp.int32, (nodes, LANES), 1)
    query = query_ref[:, at].astype(F32) * width**-0.5
    query = jnp.where(lane // width == head, query, 0.0).astype(BF16)
    start = 0
    for keys in pairs:
        count = keys.shape[0]
        score_ref[:, start : start + count] = lax.dot_general(
            query, keys[:, at], (((1,), (1,)), ((), ())), preferred_element_type=F32
        )
        start += count


def head_weights(score_ref, bias_ref, weight_ref, floor):
    nodes = score_ref.shape[0]
    peaks = []
    for start in range(0, nodes, CHUNK):
        rows = slice(start, start + CHUNK)
        scores = score_ref[rows] + bias_ref[rows]
        peak = jnp.max(scores, axis=1, keepdims=True)
        if floor is not None:
            peak = jnp.maximum(peak, floor[rows])
        weight_ref[rows] = jnp.exp(scores - peak).astype(BF16)
        peaks.append(peak)
    return jnp.concatenate(peaks, axis=0)


def head_values(weight_ref, pairs, at):
    total, start = None, 0
    for values in pairs:
        count = values.shape[0]
        rhs = jnp.concatenate([values[:, at], jnp.ones((count, LANES), BF16)], axis=1)
        part = jnp.dot(weight_ref[:, start : start + count], rhs, preferred_element_type=F32)
        total = part if total is None else total + part
        start += count
    return total[:, :LANES], total[:, LANES:]


def far_kernel(mean_ref, w_embed, w_encode, w_key, w_value, gain, *refs):
    feats, pair_ref = [feat.now() for feat in refs[:-1]], refs[-1]
    sector_rows(
        mean_ref, gain.now(), w_embed, w_encode, None, w_key, w_value, feats, None, None, pair_ref
    )


def own_kernel(
    bands, mean_ref, bias_ref, w_embed, w_encode, w_query, w_key, w_value, gain, *refs
):
    feats, refs = [feat.now() for feat in refs[:bands]], refs[bands:]
    latent_ref, query_ref, pair_ref, mixed_ref, peak_ref, sum_ref, score_ref, weight_ref = refs
    nodes, features = query_ref.shape
    sector_rows(
        mean_ref, gain.now(), w_embed, w_encode, w_query, w_key, w_value, feats,
        latent_ref, query_ref, pair_ref,
    )
    width = LANES // 2
    first = lax.broadcasted_iota(jnp.int32, (nodes, LANES), 1) < width
    per_step = score_ref.shape[0] // 2

    def attend(step, carry):
        ats = []
        for pair in range(per_step):
            base = (step * per_step + pair) * LANES
            ats.append(
                (
                    pl.ds(pl.multiple_of(base, LANES), LANES),
                    pl.ds(pl.multiple_of(base + features, LANES), LANES),
                )
            )
        for pair, (at, _) in enumerate(ats):
            for head in range(2):
                head_scores(query_ref, [pair_ref], at, head, score_ref.at[2 * pair + head])
        for pair, (at, value_at) in enumerate(ats):
            done = []
            for head in range(2):
                slot = 2 * pair + head
                peak = head_weights(score_ref.at[slot], bias_ref, weight_ref.at[slot], None)
                mixed, total = head_values(weight_ref.at[slot], [pair_ref], value_at)
                done.append((mixed, total, jnp.broadcast_to(peak, (nodes, LANES))))
            for ref, one, two in zip((mixed_ref, sum_ref, peak_ref), *done):
                ref[:, at] = jnp.where(first, one, two)
        return carry

    lax.fori_loop(0, features // LANES // per_step, attend, 0)


def attend_kernel(
    near_ref, far_ref, bias_ref, latent_ref, query_ref, mixed_ref, peak_ref, sum_ref,
    w_output, w_decode, gain_dec, w_read, out_ref, score_ref, weight_ref, context_ref,
):
    nodes, features = latent_ref.shape
    width = LANES // 2
    first = lax.broadcasted_iota(jnp.int32, (nodes, LANES), 1) < width
    per_step = score_ref.shape[0] // 2
    pairs = [near_ref, far_ref]

    def attend(step, carry):
        ats = []
        for pair in range(per_step):
            base = (step * per_step + pair) * LANES
            ats.append(
                (
                    pl.ds(pl.multiple_of(base, LANES), LANES),
                    pl.ds(pl.multiple_of(base + features, LANES), LANES),
                )
            )
        for pair, (at, _) in enumerate(ats):
            for head in range(2):
                head_scores(query_ref, pairs, at, head, score_ref.at[2 * pair + head])
        for pair, (at, value_at) in enumerate(ats):
            old_peak = peak_ref[:, at]
            done = []
            for head in range(2):
                slot = 2 * pair + head
                floor = old_peak[:, head * width : head * width + 1]
                peak = head_weights(score_ref.at[slot], bias_ref, weight_ref.at[slot], floor)
                mixed, total = head_values(weight_ref.at[slot], pairs, value_at)
                done.append((mixed, total, jnp.broadcast_to(peak, (nodes, LANES))))
            mixed, total, peak = (jnp.where(first, one, two) for one, two in zip(*done))
            fade = jnp.exp(old_peak - peak)
            mixed = mixed + fade * mixed_ref[:, at]
            total = total + fade * sum_ref[:, at]
            context_ref[:, at] = (mixed / total).astype(BF16)
        return carry

    lax.fori_loop(0, features // LANES // per_step, attend, 0)
    mixed = latent_ref[...] + jnp.dot(context_ref[...], w_output[...], preferred_element_type=F32)
    normed_out = layer_norm(mixed, gain_dec.now()[...]).astype(BF16)
    decoded = silu(jnp.dot(normed_out, w_decode[...], preferred_element_type=F32)).astype(BF16)
    out_ref[...] = lax.dot_general(
        w_read.now()[...], decoded, (((1,), (1,)), ((), ())), preferred_element_type=F32
    ).astype(BF16)


def decode_kernel(bands, sectors, nodes, parts, place_ref, dec, *refs):
    base, reads, out_ref = refs[0], refs[1:-1], refs[-1]
    dec_ref = dec.now()
    rows, cols = out_ref.shape[1:]
    iota = lax.broadcasted_iota(jnp.int32, (nodes, cols), 0).astype(F32).astype(BF16)
    one = jnp.ones((nodes, cols), BF16)
    none = jnp.zeros((nodes, cols), BF16)
    block, member = place_of(dec_ref[...], place_ref, nodes, bands, sectors)
    for row in range(rows):
        update = jnp.zeros((out_ref.shape[0], cols), F32)
        for part, (index, at) in parts:
            code = jnp.where(block[:, row] == part, member[:, row], -1.0).astype(BF16)
            counts = none
            for slot in range(code.shape[0]):
                counts = counts + jnp.where(iota == code[slot : slot + 1], one, none)
            update += jnp.dot(
                reads[index][:, at * nodes : (at + 1) * nodes], counts, preferred_element_type=F32
            )
        out_ref[:, row, :] = update / 3.0
    base = base.now() if isinstance(base, Late) else base
    out_ref[...] += base[...].astype(F32)


class Late:
    def __init__(self, source, target, semaphore):
        self.target = target
        self.copy = pltpu.make_async_copy(source, target, semaphore)
        self.copy.start()
        self.waited = False

    def now(self):
        if not self.waited:
            self.copy.wait()
            self.waited = True
        return self.target


def call(name, kernel, outs, scalars, operands, late=(), scratch=(), mib=8, micros=1):
    single = not isinstance(outs, (list, tuple))
    outs = [outs] if single else list(outs)
    n_in, n_late, n_out = len(scalars) + len(operands), len(late), len(outs)

    def run(*refs):
        ins, refs = refs[:n_in], refs[n_in:]
        sources, refs = refs[:n_late], refs[n_late:]
        results, refs = refs[:n_out], refs[n_out:]
        targets, refs = refs[:n_late], refs[n_late:]
        if n_late:
            semaphores, refs = refs[-1], refs[:-1]
        fetched = [
            Late(source, target, semaphores.at[index])
            for index, (source, target) in enumerate(zip(sources, targets))
        ]
        kernel(*ins, *fetched, *results, *refs)

    fetch = [pltpu.VMEM(a.shape, a.dtype) for a in late]
    signals = [pltpu.SemaphoreType.DMA((n_late,))] if n_late else []
    specs = [whole(pltpu.SMEM)] * len(scalars) + [whole()] * len(operands)
    specs += [whole(pltpu.HBM)] * n_late
    result = pl.pallas_call(
        run,
        name=name,
        out_shape=outs,
        in_specs=specs,
        out_specs=[whole()] * n_out,
        scratch_shapes=fetch + list(scratch) + signals,
        compiler_params=params(mib),
        cost_estimate=pl.CostEstimate(
            flops=int(micros * 5e8), bytes_accessed=int(micros * 3e6), transcendentals=0
        ),
    )(*scalars, *operands, *late)
    return result[0] if single else result


def after(value, *earlier):
    return lax.optimization_barrier((value,) + earlier)[0]


def body(
    grid_state, mesh_feat, enc_src, enc_count, nbr_ids, nbr_count, dec_src,
    w_embed, w_encode, w_query, w_key, w_value, w_output, w_decode, w_readout, norm_attn, norm_dec,
):
    shape = jax.ShapeDtypeStruct
    bands, sectors = lax.axis_size("lat"), lax.axis_size("lon")
    place = jnp.stack([lax.axis_index("lat"), lax.axis_index("lon")]).astype(jnp.int32)
    variables, rows, cols = grid_state.shape
    nodes, features = mesh_feat.shape
    slots = enc_src.shape[0]
    cells, rim = rows * cols, rows * HALO
    sector_nodes = bands * nodes

    flat, near_rim, far_rim, live = call(
        "prep",
        prep_kernel,
        [
            shape((variables, cells), BF16),
            shape((variables, rim), BF16),
            shape((variables, rim), BF16),
            shape((slots, nodes), jnp.int32),
        ],
        (place,),
        (),
        late=(grid_state, enc_src, enc_count[None]),
        scratch=[pltpu.VMEM((variables, rows, cols), F32)],
        micros=2,
    )
    far_rim = from_far(far_rim)
    lives = [live] + from_bands(live)
    near_rim = from_near(near_rim)

    encoded = []
    for step, source in enumerate(lives):
        encoded += call(
            "encode",
            encode_kernel,
            [shape((variables, nodes), F32), shape((2 * rim, nodes), BF16)],
            (place,),
            (source, flat),
            scratch=[pltpu.VMEM((cells, nodes), BF16)],
            micros=0.1 if step else 3,
        )
    feat = after(mesh_feat, encoded[0])
    feats = [feat] + from_bands(feat)
    feat_far = from_far(feat)
    summed = call(
        "rim", rim_kernel, shape((variables, sector_nodes), F32), (),
        (near_rim, far_rim, *encoded), micros=0.1,
    )
    received = from_bands(summed)
    bias_own, bias_rest = call(
        "bias",
        functools.partial(bias_kernel, bands, sectors),
        [shape((nodes, sector_nodes), F32), shape((nodes, 2 * sector_nodes), F32)],
        (place,),
        (),
        late=(after(nbr_ids, summed), nbr_count[None]),
        micros=30,
    )
    mean = call(
        "mean",
        mean_kernel,
        shape((variables, sector_nodes), BF16),
        (),
        (after(summed, bias_own, *feats, feat_far), *received, *lives),
        micros=0.1,
    )
    feats_far = [feat_far] + from_bands(feat_far)
    mean_far = from_far(mean)
    latent, query, pair, mixed, peak, total = call(
        "own",
        functools.partial(own_kernel, bands),
        [
            shape((nodes, features), F32),
            shape((nodes, features), BF16),
            shape((sector_nodes, 2 * features), BF16),
        ]
        + [shape((nodes, features), F32)] * 3,
        (),
        (mean, bias_own, w_embed, w_encode, w_query, w_key, w_value),
        late=(norm_attn[None], *feats),
        scratch=[
            pltpu.VMEM((4, nodes, sector_nodes), F32),
            pltpu.VMEM((4, nodes, sector_nodes), BF16),
        ],
        mib=30,
        micros=10,
    )
    pair_near = from_near(pair)
    pair_far = call(
        "far",
        far_kernel,
        shape((sector_nodes, 2 * features), BF16),
        (),
        (mean_far, after(w_embed, pair), w_encode, w_key, w_value),
        late=(norm_attn[None], *feats_far),
        mib=16,
        micros=60,
    )
    readout = call(
        "attend",
        attend_kernel,
        shape((variables, nodes), BF16),
        (),
        (pair_near, pair_far, bias_rest, latent, query, mixed, peak, total, w_output, w_decode),
        late=(norm_dec[None], w_readout.T),
        scratch=[
            pltpu.VMEM((4, nodes, 2 * sector_nodes), F32),
            pltpu.VMEM((4, nodes, 2 * sector_nodes), BF16),
            pltpu.VMEM((nodes, features), BF16),
        ],
        mib=28,
        micros=12,
    )
    banded = from_bands(readout)
    reads = jnp.concatenate([readout] + banded, axis=1)
    read_far = from_far(reads)
    read_near = from_near(reads)
    kernel = functools.partial(decode_kernel, bands, sectors, nodes)
    result = shape(grid_state.shape, F32)

    sums = call(
        "decode_own",
        lambda place_ref, read_ref, dec, grid, out_ref: kernel(
            [(0, (0, 0))], place_ref, dec, grid, read_ref, out_ref
        ),
        result,
        (place,),
        (readout,),
        late=(dec_src, grid_state),
        micros=0.1,
    )
    near_parts = [(band, (0, band)) for band in range(1, bands)]
    near_parts += [(bands + band, (1, band)) for band in range(bands)]
    sums = call(
        "decode_near",
        lambda place_ref, sum_ref, own_ref, near_ref, dec, out_ref: kernel(
            near_parts, place_ref, dec, sum_ref, own_ref, near_ref, out_ref
        ),
        result,
        (place,),
        (sums, reads, read_near),
        late=(dec_src,),
        micros=0.1,
    )
    far_parts = [(2 * bands + band, (0, band)) for band in range(bands)]
    return call(
        "decode_far",
        lambda place_ref, sum_ref, far_ref, dec, out_ref: kernel(
            far_parts, place_ref, dec, sum_ref, far_ref, out_ref
        ),
        result,
        (place,),
        (sums, read_far),
        late=(dec_src,),
        micros=0.1,
    )


def solution(mesh):
    in_specs = (
        P(None, "lat", "lon"),
        P(("lat", "lon"), None),
        P(None, ("lat", "lon")),
        P(("lat", "lon")),
        P(None, ("lat", "lon")),
        P(("lat", "lon")),
        P(None, "lat", "lon"),
    ) + (P(),) * 10
    out_specs = P(None, "lat", "lon")
    return jax.shard_map(body, mesh=mesh, in_specs=in_specs, out_specs=out_specs, check_vma=False)
```

```python
import functools

import jax
import jax.numpy as jnp
from jax import lax
from jax.experimental import pallas as pl
from jax.experimental.pallas import tpu as pltpu
from jax.sharding import PartitionSpec as P

HEADS = 16
HALO = 16
BF16 = jnp.bfloat16
F32 = jnp.float32
MIB = 1024 * 1024


def params(mib):
    return pltpu.CompilerParams(vmem_limit_bytes=mib * MIB)


def whole(memory=pltpu.VMEM):
    return pl.BlockSpec(memory_space=memory)


def silu(value):
    return 0.5 * value * (1.0 + jnp.tanh(0.5 * value))


def layer_norm(inputs_f, gain):
    centre = inputs_f - jnp.mean(inputs_f, axis=-1, keepdims=True)
    spread = jnp.mean(centre * centre, axis=-1, keepdims=True)
    return centre * lax.rsqrt(spread + 1e-05) * gain


def from_bands(value):
    count = lax.axis_size("lat")
    return [
        lax.ppermute(value, "lat", [(i, (i - step) % count) for i in range(count)])
        for step in range(1, count)
    ]


def from_near(value):
    count = lax.axis_size("lon")
    return lax.ppermute(value, "lon", [(i, i ^ 1) for i in range(count)])


def from_far(value):
    count = lax.axis_size("lon")
    return lax.ppermute(value, "lon", [(i, (i - 1 + 2 * (i % 2)) % count) for i in range(count)])


def quotient(value_f, divisor):
    return jnp.floor((value_f + 0.5) * (1.0 / divisor))


def prep_kernel(grid, src, count, near_ref, far_ref, live_ref, wide):
    slot = lax.broadcasted_iota(jnp.int32, live_ref.shape, 0)
    live_ref[...] = jnp.where(slot < count.now()[...], src.now()[...], -1)
    grid_ref = grid.now()
    rows, cols = grid_ref.shape[1:]
    per_tile = cols // HALO
    odd = lax.axis_index("lon") % 2
    near_at = jnp.where(odd == 0, cols - HALO, 0)
    far_at = cols - HALO - near_at
    lane = lax.broadcasted_iota(jnp.int32, (grid_ref.shape[0], cols), 1) // HALO
    wide[...] = grid_ref[...].astype(F32)
    for tile in range(rows // per_tile):
        near, far = None, None
        for place in range(per_tile):
            line = wide[:, tile * per_tile + place, :]
            turned = [
                pltpu.roll(line, (place * HALO - start + cols) % cols, 1)
                for start in (near_at, far_at)
            ]
            near = turned[0] if near is None else jnp.where(lane == place, turned[0], near)
            far = turned[1] if far is None else jnp.where(lane == place, turned[1], far)
        near_ref[:, tile * cols : (tile + 1) * cols] = near.astype(BF16)
        far_ref[:, tile * cols : (tile + 1) * cols] = far.astype(BF16)


def flat_kernel(grid, flat_ref, wide):
    grid_ref = grid.now()
    rows, cols = grid_ref.shape[1:]
    wide[...] = grid_ref[...].astype(F32)
    for row in range(rows):
        flat_ref[:, row * cols : (row + 1) * cols] = wide[:, row, :].astype(BF16)


def encode_kernel(src_ref, flat_ref, out_ref, rim_ref, counts):
    slots, nodes = src_ref.shape
    cells = flat_ref.shape[1]
    rim = rim_ref.shape[0] // 2
    rows = rim // HALO
    cols = cells // rows
    span = cols + 2 * HALO
    lanes = 128
    even = lax.axis_index("lon") % 2 == 0
    source = src_ref[...].astype(F32)
    row_of = quotient(source, span)
    col_of = source - row_of * span
    row_of = row_of - (lax.axis_index("lat") * rows).astype(F32)
    iota = lax.broadcasted_iota(jnp.int32, (span, lanes), 0).astype(F32).astype(BF16)
    one = jnp.ones((span, lanes), BF16)
    none = jnp.zeros((span, lanes), BF16)
    west = pl.multiple_of(jnp.where(even, rim, 0), rim)
    east = pl.multiple_of(jnp.where(even, 0, rim), rim)
    for row in range(rows):
        code = jnp.where(row_of == row, col_of, -1.0).astype(BF16)
        for tile in range(nodes // lanes):
            at = slice(tile * lanes, (tile + 1) * lanes)
            total = none
            for slot in range(slots):
                total = total + jnp.where(iota == code[slot : slot + 1, at], one, none)
            counts[row * cols : (row + 1) * cols, at] = total[HALO : HALO + cols]
            rim_ref[pl.ds(west + row * HALO, HALO), at] = total[:HALO]
            rim_ref[pl.ds(east + row * HALO, HALO), at] = total[HALO + cols :]
        if row % 2 == 1:
            part = slice((row - 1) * cols, (row + 1) * cols)
            summed = jnp.dot(flat_ref[:, part], counts[part], preferred_element_type=F32)
            out_ref[...] = summed if row == 1 else out_ref[...] + summed


def rim_kernel(near_ref, far_ref, *refs):
    out_ref = refs[-1]
    rim = near_ref.shape[1]
    for part in range(len(refs) // 2):
        summed, counts = refs[2 * part], refs[2 * part + 1]
        nodes = summed.shape[1]
        total = summed[...]
        total += jnp.dot(near_ref[...], counts[:rim], preferred_element_type=F32)
        total += jnp.dot(far_ref[...], counts[rim:], preferred_element_type=F32)
        out_ref[:, part * nodes : (part + 1) * nodes] = total


def mean_kernel(own_ref, *refs):
    out_ref = refs[-1]
    bands = len(refs) // 2
    others, sources = refs[: bands - 1], refs[bands - 1 : -1]
    nodes = own_ref.shape[1] // bands
    for band in range(bands):
        at = slice(band * nodes, (band + 1) * nodes)
        count = jnp.sum(jnp.where(sources[band][...] >= 0, 1.0, 0.0), axis=0, keepdims=True)
        total = own_ref[:, at]
        for step, other in enumerate(others, 1):
            there = (band - step) % bands
            total = total + other[:, there * nodes : (there + 1) * nodes]
        out_ref[:, at] = (total / count).astype(BF16)


def place_of(ids, node_count, bands, sectors):
    ids_f = ids.astype(F32)
    device = quotient(ids_f, node_count)
    member = ids_f - device * node_count
    band = quotient(device, sectors)
    sector = device - band * sectors
    mine = lax.axis_index("lon")
    near = mine + 1 - 2 * (mine % 2)
    side = jnp.where(sector == mine.astype(F32), 0.0, 2.0)
    side = jnp.where(sector == near.astype(F32), 1.0, side)
    band = band - lax.axis_index("lat").astype(F32)
    band = jnp.where(band < 0, band + bands, band)
    return side * bands + band, member


def bias_kernel(bands, sectors, ids, count, own_ref, rest_ref):
    ids_ref, count_ref = ids.now(), count.now()
    slots, nodes = ids_ref.shape
    lanes = 128
    block, member = place_of(ids_ref[...], nodes, bands, sectors)
    slot_of = lax.broadcasted_iota(jnp.int32, (slots, nodes), 0)
    block = jnp.where(slot_of < count_ref[...], block, -1.0)
    iota = lax.broadcasted_iota(jnp.int32, (nodes, lanes), 0).astype(F32).astype(BF16)
    shut = jnp.full((nodes, lanes), -1e30, BF16)
    opened = jnp.zeros((nodes, lanes), BF16)
    for part in range(3 * bands):
        code = jnp.where(block == part, member, -1.0).astype(BF16)
        ref, index = (own_ref, part) if part < bands else (rest_ref, part - bands)
        for tile in range(nodes // lanes):
            at = slice(tile * lanes, (tile + 1) * lanes)
            total = shut
            for slot in range(slots):
                total = jnp.where(iota == code[slot : slot + 1, at], opened, total)
            ref[at, index * nodes : (index + 1) * nodes] = total.astype(F32).T


def latent_of(mean, feat, w_embed, w_encode):
    embedded = silu(
        lax.dot_general(mean, w_embed, (((0,), (0,)), ((), ())), preferred_element_type=F32)
    ).astype(BF16)
    return feat.astype(F32) + jnp.dot(embedded, w_encode, preferred_element_type=F32)


def sector_rows(
    mean_ref, gain_ref, w_embed, w_encode, w_query, w_key, w_value, feats, latent_ref, query_ref, pair_ref
):
    nodes, features = feats[0].shape
    normed = []
    for part, feat in enumerate(feats):
        at = slice(part * nodes, (part + 1) * nodes)
        latent = latent_of(mean_ref[:, at], feat[...], w_embed[...], w_encode[...])
        normed.append(layer_norm(latent, gain_ref[...]).astype(BF16))
        if part == 0 and latent_ref is not None:
            latent_ref[...] = latent
            query_ref[...] = jnp.dot(
                normed[0], w_query[...], preferred_element_type=F32
            ).astype(BF16)
    normed = jnp.concatenate(normed, axis=0)
    pair_ref[:, :features] = jnp.dot(normed, w_key[...], preferred_element_type=F32).astype(BF16)
    pair_ref[:, features:] = jnp.dot(normed, w_value[...], preferred_element_type=F32).astype(BF16)


LANES = 128
CHUNK = 32
SLOTS = 2
PREP_MIB = 62


def pair_scores(query_ref, pairs, at, score_ref):
    nodes = query_ref.shape[0]
    width = LANES // 2
    first = lax.broadcasted_iota(jnp.int32, (nodes, LANES), 1) < width
    query = query_ref[:, at].astype(F32) * width**-0.5
    query = jnp.concatenate(
        [jnp.where(first, query, 0.0).astype(BF16), jnp.where(first, 0.0, query).astype(BF16)], axis=0
    )
    start = 0
    for keys in pairs:
        count = keys.shape[0]
        score_ref[:, start : start + count] = lax.dot_general(
            query, keys[:, at], (((1,), (1,)), ((), ())), preferred_element_type=F32
        )
        start += count


def pair_weights(score_ref, bias_ref, weight_ref, floors):
    nodes = bias_ref.shape[0]
    peaks = []
    for start in range(0, 2 * nodes, CHUNK):
        rows = slice(start, start + CHUNK)
        there = slice(start % nodes, start % nodes + CHUNK)
        scores = score_ref[rows] + bias_ref[there]
        peak = jnp.max(scores, axis=1, keepdims=True)
        if floors is not None:
            peak = jnp.maximum(peak, floors[start // nodes][there])
        weight_ref[rows] = jnp.exp(scores - peak).astype(BF16)
        peaks.append(jnp.broadcast_to(peak, (CHUNK, LANES)))
    return jnp.concatenate(peaks, axis=0)


def pair_values(weight_ref, pairs, at):
    total, start = None, 0
    for values in pairs:
        count = values.shape[0]
        rhs = jnp.concatenate([values[:, at], jnp.ones((count, LANES), BF16)], axis=1)
        part = jnp.dot(weight_ref[:, start : start + count], rhs, preferred_element_type=F32)
        total = part if total is None else total + part
        start += count
    return total[:, :LANES], total[:, LANES:]


def attention(query_ref, pairs, bias_ref, score_ref, weight_ref, peak_ref, store):
    nodes, features = query_ref.shape
    width = LANES // 2
    first = lax.broadcasted_iota(jnp.int32, (nodes, LANES), 1) < width
    ats = [slice(base, base + LANES) for base in range(0, features, LANES)]
    slots = score_ref.shape[0]
    for pair in range(min(slots - 1, len(ats))):
        pair_scores(query_ref, pairs, ats[pair], score_ref.at[pair])
    for pair, at in enumerate(ats):
        ahead = pair + slots - 1
        if ahead < len(ats):
            pair_scores(query_ref, pairs, ats[ahead], score_ref.at[ahead % slots])
        floors = None
        if peak_ref is not None:
            old = peak_ref[:, at]
            floors = [old[:, :1], old[:, width : width + 1]]
        slot = pair % slots
        peaks = pair_weights(score_ref.at[slot], bias_ref, weight_ref.at[slot], floors)
        value_at = slice(at.start + features, at.stop + features)
        values, sums = pair_values(weight_ref.at[slot], pairs, value_at)
        store(at, *(jnp.where(first, a[:nodes], a[nodes:]) for a in (values, sums, peaks)))


def far_kernel(mean_ref, w_embed, w_encode, w_key, w_value, gain, *refs):
    feats, pair_ref = [feat.now() for feat in refs[:-1]], refs[-1]
    sector_rows(
        mean_ref, gain.now(), w_embed, w_encode, None, w_key, w_value, feats, None, None, pair_ref
    )


def own_kernel(
    bands, mean_ref, bias_ref, w_embed, w_encode, w_query, w_key, w_value, gain, *refs
):
    feats, refs = [feat.now() for feat in refs[:bands]], refs[bands:]
    latent_ref, query_ref, pair_ref, mixed_ref, peak_ref, sum_ref, score_ref, weight_ref = refs
    nodes, features = query_ref.shape
    sector_rows(
        mean_ref, gain.now(), w_embed, w_encode, w_query, w_key, w_value, feats,
        latent_ref, query_ref, pair_ref,
    )

    def store(at, values, sums, peaks):
        mixed_ref[:, at] = values
        sum_ref[:, at] = sums
        peak_ref[:, at] = peaks

    attention(query_ref, [pair_ref], bias_ref, score_ref, weight_ref, None, store)


def attend_kernel(
    near_ref, far_ref, bias_ref, latent_ref, query_ref, mixed_ref, peak_ref, sum_ref,
    w_output, w_decode, gain_dec, w_read, out_ref, score_ref, weight_ref, context_ref,
):
    nodes, features = latent_ref.shape

    def store(at, values, sums, peaks):
        fade = jnp.exp(peak_ref[:, at] - peaks)
        values = values + fade * mixed_ref[:, at]
        context_ref[:, at] = (values / (sums + fade * sum_ref[:, at])).astype(BF16)

    attention(query_ref, [near_ref, far_ref], bias_ref, score_ref, weight_ref, peak_ref, store)
    mixed = latent_ref[...] + jnp.dot(context_ref[...], w_output[...], preferred_element_type=F32)
    normed_out = layer_norm(mixed, gain_dec.now()[...]).astype(BF16)
    decoded = silu(jnp.dot(normed_out, w_decode[...], preferred_element_type=F32)).astype(BF16)
    out_ref[...] = lax.dot_general(
        w_read.now()[...], decoded, (((1,), (1,)), ((), ())), preferred_element_type=F32
    ).astype(BF16)


def decode_kernel(bands, sectors, parts, dec, reads, base_ref, out_ref, wide=None, signals=None):
    dec_ref = dec.now()
    rows, cols = dec_ref.shape[1:]
    nodes = parts[0][1].stop - parts[0][1].start
    iota = lax.broadcasted_iota(jnp.int32, (nodes, 2 * cols), 0).astype(F32).astype(BF16)
    one = jnp.ones((nodes, 2 * cols), BF16)
    none = jnp.zeros((nodes, 2 * cols), BF16)
    block, member = place_of(dec_ref[...], nodes, bands, sectors)
    copies, half = [], rows // 2
    for row in range(0, rows, 2):
        at = slice(row * cols, (row + 2) * cols)
        update = None
        for (part, there), read_ref in zip(parts, reads):
            code = jnp.where(block == part, member, -1.0)
            code = jnp.concatenate([code[:, row], code[:, row + 1]], axis=1).astype(BF16)
            counts = none
            for slot in range(code.shape[0]):
                counts = counts + jnp.where(iota == code[slot : slot + 1], one, none)
            share = jnp.dot(read_ref[:, there], counts, preferred_element_type=F32)
            update = share if update is None else update + share
        update = base_ref[:, at].astype(F32) + update / 3.0
        if wide is None:
            out_ref[:, at] = update
            continue
        wide[:, row, :] = update[:, :cols]
        wide[:, row + 1, :] = update[:, cols:]
        if (row + 2) % half == 0:
            done = slice(row + 2 - half, row + 2)
            copies.append(
                pltpu.make_async_copy(
                    wide.at[:, done], out_ref.at[:, done], signals.at[len(copies)]
                )
            )
            copies[-1].start()
    for copy in copies:
        copy.wait()


class Late:
    def __init__(self, source, target, semaphore):
        self.target = target
        self.copy = pltpu.make_async_copy(source, target, semaphore)
        self.copy.start()
        self.waited = False

    def now(self):
        if not self.waited:
            self.copy.wait()
            self.waited = True
        return self.target


def call(name, kernel, outs, operands, late=(), scratch=(), mib=8, micros=1, out_memory=pltpu.VMEM):
    single = not isinstance(outs, (list, tuple))
    outs = [outs] if single else list(outs)
    n_in, n_late, n_out = len(operands), len(late), len(outs)

    def run(*refs):
        ins, refs = refs[:n_in], refs[n_in:]
        sources, refs = refs[:n_late], refs[n_late:]
        results, refs = refs[:n_out], refs[n_out:]
        targets, refs = refs[:n_late], refs[n_late:]
        if n_late:
            semaphores, refs = refs[0], refs[1:]
        fetched = [
            Late(source, target, semaphores.at[index])
            for index, (source, target) in enumerate(zip(sources, targets))
        ]
        kernel(*ins, *fetched, *results, *refs)

    fetch = [pltpu.VMEM(a.shape, a.dtype) for a in late]
    signals = [pltpu.SemaphoreType.DMA((n_late,))] if n_late else []
    specs = [whole()] * n_in + [whole(pltpu.HBM)] * n_late
    result = pl.pallas_call(
        run,
        name=name,
        out_shape=outs,
        in_specs=specs,
        out_specs=[whole(out_memory)] * n_out,
        scratch_shapes=fetch + signals + list(scratch),
        compiler_params=params(mib),
        cost_estimate=pl.CostEstimate(
            flops=int(micros * 5e8), bytes_accessed=int(micros * 3e6), transcendentals=0
        ),
    )(*operands, *late)
    return result[0] if single else result


def after(value, *earlier):
    return lax.optimization_barrier((value,) + earlier)[0]


def body(
    grid_state, mesh_feat, enc_src, enc_count, nbr_ids, nbr_count, dec_src,
    w_embed, w_encode, w_query, w_key, w_value, w_output, w_decode, w_readout, norm_attn, norm_dec,
):
    shape = jax.ShapeDtypeStruct
    bands, sectors = lax.axis_size("lat"), lax.axis_size("lon")
    variables, rows, cols = grid_state.shape
    nodes, features = mesh_feat.shape
    slots = enc_src.shape[0]
    cells, rim = rows * cols, rows * HALO
    sector_nodes = bands * nodes

    near_rim, far_rim, live = call(
        "prep",
        prep_kernel,
        [
            shape((variables, rim), BF16),
            shape((variables, rim), BF16),
            shape((slots, nodes), jnp.int32),
        ],
        (),
        late=(grid_state, enc_src, enc_count[None]),
        scratch=[pltpu.VMEM((variables, rows, cols), F32)],
        mib=PREP_MIB,
        micros=2,
    )
    feat = after(mesh_feat, live)
    far_rim = from_far(far_rim)
    lives = [live] + from_bands(live)
    near_rim = from_near(near_rim)
    flat = call(
        "flat",
        flat_kernel,
        shape((variables, cells), BF16),
        (),
        late=(after(grid_state, live),),
        scratch=[pltpu.VMEM((variables, rows, cols), F32)],
        micros=0.1,
    )
    encoded = []
    for step, source in enumerate(lives):
        encoded += call(
            "encode",
            encode_kernel,
            [shape((variables, nodes), F32), shape((2 * rim, nodes), BF16)],
                (source, flat),
            scratch=[pltpu.VMEM((cells, nodes), BF16)],
            micros=0.1 if step else 3,
        )
    feats = [feat] + from_bands(feat)
    feat_far = from_far(feat)
    summed = call(
        "rim", rim_kernel, shape((variables, sector_nodes), F32),
        (near_rim, far_rim, *encoded), micros=0.1,
    )
    received = from_bands(summed)
    bias_own, bias_rest = call(
        "bias",
        functools.partial(bias_kernel, bands, sectors),
        [shape((nodes, sector_nodes), F32), shape((nodes, 2 * sector_nodes), F32)],
        (),
        late=(after(nbr_ids, summed), nbr_count[None]),
        micros=30,
    )
    mean = call(
        "mean",
        mean_kernel,
        shape((variables, sector_nodes), BF16),
        (after(summed, bias_own), *received, *lives),
        micros=0.1,
    )
    feats_far = [feat_far] + from_bands(after(feat_far, mean))
    mean_far = from_far(mean)
    latent, query, pair, mixed, peak, total = call(
        "own",
        functools.partial(own_kernel, bands),
        [
            shape((nodes, features), F32),
            shape((nodes, features), BF16),
            shape((sector_nodes, 2 * features), BF16),
        ]
        + [shape((nodes, features), F32)] * 3,
        (mean, bias_own, after(w_embed, feat_far), w_encode, w_query, w_key, w_value),
        late=(norm_attn[None], *feats),
        scratch=[
            pltpu.VMEM((SLOTS, 2 * nodes, sector_nodes), F32),
            pltpu.VMEM((SLOTS, 2 * nodes, sector_nodes), BF16),
        ],
        mib=30,
        micros=10,
    )
    pair_near = from_near(pair)
    pair_far = call(
        "far",
        far_kernel,
        shape((sector_nodes, 2 * features), BF16),
        (mean_far, after(w_embed, pair), w_encode, w_key, w_value),
        late=(norm_attn[None], *feats_far),
        mib=16,
        micros=60,
    )
    readout = call(
        "attend",
        attend_kernel,
        shape((variables, nodes), BF16),
        (pair_near, pair_far, bias_rest, latent, query, mixed, peak, total, w_output, w_decode),
        late=(norm_dec[None], w_readout.T),
        scratch=[
            pltpu.VMEM((SLOTS, 2 * nodes, 2 * sector_nodes), F32),
            pltpu.VMEM((SLOTS, 2 * nodes, 2 * sector_nodes), BF16),
            pltpu.VMEM((nodes, features), BF16),
        ],
        mib=28,
        micros=12,
    )
    sums = shape((variables, cells), F32)
    decode = functools.partial(decode_kernel, bands, sectors)
    spots = [slice(band * nodes, (band + 1) * nodes) for band in range(bands)]
    own_sums = call(
        "decode_own",
        lambda read, base, dec, out: decode([(0, spots[0])], dec, [read], base, out),
        sums,
        (readout, flat),
        late=(dec_src,),
        micros=0.1,
    )
    reads = jnp.concatenate([readout] + from_bands(readout), axis=1)
    reads = after(reads, own_sums)
    read_far = from_far(reads)
    read_near = from_near(reads)
    near_sums = call(
        "decode_near",
        lambda base, own, near, dec, out: decode(
            list(enumerate(spots))[1:] + list(enumerate(spots, bands)),
            dec, [own] * (bands - 1) + [near] * bands, base, out,
        ),
        sums,
        (own_sums, reads, read_near),
        late=(dec_src,),
        micros=0.1,
    )
    return call(
        "decode_far",
        lambda base, far, dec, out, *more: decode(
            list(enumerate(spots, 2 * bands)), dec, [far] * bands, base, out, *more
        ),
        shape(grid_state.shape, F32),
        (near_sums, read_far),
        late=(dec_src,),
        scratch=[pltpu.VMEM(grid_state.shape, F32), pltpu.SemaphoreType.DMA((2,))],
        out_memory=pltpu.HBM,
        micros=0.1,
    )


def solution(mesh):
    in_specs = (
        P(None, "lat", "lon"),
        P(("lat", "lon"), None),
        P(None, ("lat", "lon")),
        P(("lat", "lon")),
        P(None, ("lat", "lon")),
        P(("lat", "lon")),
        P(None, "lat", "lon"),
    ) + (P(),) * 10
    out_specs = P(None, "lat", "lon")
    return jax.shard_map(body, mesh=mesh, in_specs=in_specs, out_specs=out_specs, check_vma=False)
```

```python
import functools

import jax
import jax.numpy as jnp
from jax import lax
from jax.experimental import pallas as pl
from jax.experimental.pallas import tpu as pltpu
from jax.sharding import PartitionSpec as P

HEADS = 16
HALO = 16
BF16 = jnp.bfloat16
F32 = jnp.float32
MIB = 1024 * 1024


def params(mib):
    return pltpu.CompilerParams(vmem_limit_bytes=mib * MIB)


def whole(memory=pltpu.VMEM):
    return pl.BlockSpec(memory_space=memory)


def silu(value):
    return 0.5 * value * (1.0 + jnp.tanh(0.5 * value))


def layer_norm(inputs_f, gain):
    centre = inputs_f - jnp.mean(inputs_f, axis=-1, keepdims=True)
    spread = jnp.mean(centre * centre, axis=-1, keepdims=True)
    return centre * lax.rsqrt(spread + 1e-05) * gain


def from_bands(value):
    count = lax.axis_size("lat")
    return [
        lax.ppermute(value, "lat", [(i, (i - step) % count) for i in range(count)])
        for step in range(1, count)
    ]


def from_near(value):
    count = lax.axis_size("lon")
    return lax.ppermute(value, "lon", [(i, i ^ 1) for i in range(count)])


def from_far(value):
    count = lax.axis_size("lon")
    return lax.ppermute(value, "lon", [(i, (i - 1 + 2 * (i % 2)) % count) for i in range(count)])


def quotient(value_f, divisor):
    return jnp.floor((value_f + 0.5) * (1.0 / divisor))


def first_kernel(out_ref):
    out_ref[...] = jnp.zeros(out_ref.shape, F32)


def prep_kernel(first_ref, grid_ref, src_ref, count_ref, near_ref, far_ref, live_ref, wide):
    slot = lax.broadcasted_iota(jnp.int32, live_ref.shape, 0)
    live_ref[...] = jnp.where(slot < count_ref[...], src_ref[...], -1)
    rows, cols = grid_ref.shape[1:]
    per_tile = cols // HALO
    odd = lax.axis_index("lon") % 2
    near_at = jnp.where(odd == 0, cols - HALO, 0)
    far_at = cols - HALO - near_at
    lane = lax.broadcasted_iota(jnp.int32, (grid_ref.shape[0], cols), 1) // HALO
    wide[...] = grid_ref[...].astype(F32)
    for tile in range(rows // per_tile):
        near, far = None, None
        for place in range(per_tile):
            line = wide[:, tile * per_tile + place, :]
            turned = [
                pltpu.roll(line, (place * HALO - start + cols) % cols, 1)
                for start in (near_at, far_at)
            ]
            near = turned[0] if near is None else jnp.where(lane == place, turned[0], near)
            far = turned[1] if far is None else jnp.where(lane == place, turned[1], far)
        near_ref[:, tile * cols : (tile + 1) * cols] = near.astype(BF16)
        far_ref[:, tile * cols : (tile + 1) * cols] = far.astype(BF16)


def flat_kernel(grid_ref, flat_ref, wide):
    rows, cols = grid_ref.shape[1:]
    wide[...] = grid_ref[...].astype(F32)
    for row in range(rows):
        flat_ref[:, row * cols : (row + 1) * cols] = wide[:, row, :].astype(BF16)


def encode_kernel(src_ref, flat_ref, out_ref, rim_ref):
    slots, nodes = src_ref.shape
    cells = flat_ref.shape[1]
    rim = rim_ref.shape[0] // 2
    rows = rim // HALO
    cols = cells // rows
    span = cols + 2 * HALO
    lanes = 128
    even = lax.axis_index("lon") % 2 == 0
    source = src_ref[...].astype(F32)
    row_of = quotient(source, span)
    col_of = source - row_of * span
    row_of = row_of - (lax.axis_index("lat") * rows).astype(F32)
    iota = lax.broadcasted_iota(jnp.int32, (span, lanes), 0).astype(F32).astype(BF16)
    one = jnp.ones((span, lanes), BF16)
    none = jnp.zeros((span, lanes), BF16)
    west = pl.multiple_of(jnp.where(even, rim, 0), rim)
    east = pl.multiple_of(jnp.where(even, 0, rim), rim)
    summed = None
    for row in range(0, rows, 2):
        parts = []
        for r in (row, row + 1):
            code = jnp.where(row_of == r, col_of, -1.0).astype(BF16)
            line = []
            for tile in range(nodes // lanes):
                at = slice(tile * lanes, (tile + 1) * lanes)
                total = none
                for slot in range(slots):
                    total = total + jnp.where(iota == code[slot : slot + 1, at], one, none)
                rim_ref[pl.ds(west + r * HALO, HALO), at] = total[:HALO]
                rim_ref[pl.ds(east + r * HALO, HALO), at] = total[HALO + cols :]
                line.append(total[HALO : HALO + cols])
            parts.append(jnp.concatenate(line, axis=1))
        part = slice(row * cols, (row + 2) * cols)
        got = jnp.dot(flat_ref[:, part], jnp.concatenate(parts, axis=0), preferred_element_type=F32)
        summed = got if summed is None else summed + got
    out_ref[...] = summed


def rim_kernel(near_ref, far_ref, *refs):
    out_ref, sent_ref = refs[-2:]
    rim = near_ref.shape[1]
    for part in range(len(refs) // 2 - 1):
        summed, counts = refs[2 * part], refs[2 * part + 1]
        nodes = summed.shape[1]
        total = summed[...]
        total += jnp.dot(near_ref[...], counts[:rim], preferred_element_type=F32)
        total += jnp.dot(far_ref[...], counts[rim:], preferred_element_type=F32)
        out_ref[:, part * nodes : (part + 1) * nodes] = total
    sent_ref[...] = out_ref[...].astype(BF16)


def mean_kernel(own_ref, *refs):
    out_ref = refs[-1]
    bands = len(refs) // 2
    others, sources = refs[: bands - 1], refs[bands - 1 : -1]
    nodes = own_ref.shape[1] // bands
    for band in range(bands):
        at = slice(band * nodes, (band + 1) * nodes)
        count = jnp.sum(jnp.where(sources[band][...] >= 0, 1.0, 0.0), axis=0, keepdims=True)
        total = own_ref[:, at]
        for step, other in enumerate(others, 1):
            there = (band - step) % bands
            total = total + other[:, there * nodes : (there + 1) * nodes].astype(F32)
        out_ref[:, at] = (total / count).astype(BF16)


def place_of(ids, node_count, bands, sectors):
    ids_f = ids.astype(F32)
    device = quotient(ids_f, node_count)
    member = ids_f - device * node_count
    band = quotient(device, sectors)
    sector = device - band * sectors
    mine = lax.axis_index("lon")
    near = mine + 1 - 2 * (mine % 2)
    side = jnp.where(sector == mine.astype(F32), 0.0, 2.0)
    side = jnp.where(sector == near.astype(F32), 1.0, side)
    band = band - lax.axis_index("lat").astype(F32)
    band = jnp.where(band < 0, band + bands, band)
    return side * bands + band, member


def bias_kernel(bands, sectors, ids, count, own_ref, rest_ref):
    ids_ref, count_ref = ids.now(), count.now()
    slots, nodes = ids_ref.shape
    lanes = 128
    block, member = place_of(ids_ref[...], nodes, bands, sectors)
    slot_of = lax.broadcasted_iota(jnp.int32, (slots, nodes), 0)
    block = jnp.where(slot_of < count_ref[...], block, -1.0)
    iota = lax.broadcasted_iota(jnp.int32, (nodes, lanes), 0).astype(F32).astype(BF16)
    shut = jnp.full((nodes, lanes), -1e30, BF16)
    opened = jnp.zeros((nodes, lanes), BF16)
    for part in range(3 * bands):
        code = jnp.where(block == part, member, -1.0).astype(BF16)
        ref, index = (own_ref, part) if part < bands else (rest_ref, part - bands)
        for tile in range(nodes // lanes):
            at = slice(tile * lanes, (tile + 1) * lanes)
            total = shut
            for slot in range(slots):
                total = jnp.where(iota == code[slot : slot + 1, at], opened, total)
            ref[at, index * nodes : (index + 1) * nodes] = total.astype(F32).T


def latent_of(mean, feat, w_embed, w_encode):
    embedded = silu(
        lax.dot_general(mean, w_embed, (((0,), (0,)), ((), ())), preferred_element_type=F32)
    ).astype(BF16)
    return feat.astype(F32) + jnp.dot(embedded, w_encode, preferred_element_type=F32)


def sector_rows(
    mean_ref, gain_ref, w_embed, w_encode, w_query, w_key, w_value, feats, latent_ref, query_ref, pair_ref
):
    features = feats[0].shape[1]
    normed, start = [], 0
    for part, feat in enumerate(feats):
        at = slice(start, start + feat.shape[0])
        start = at.stop
        latent = latent_of(mean_ref[:, at], feat[...], w_embed[...], w_encode[...])
        normed.append(layer_norm(latent, gain_ref[...]).astype(BF16))
        if part == 0 and latent_ref is not None:
            latent_ref[...] = latent
            query_ref[...] = jnp.dot(
                normed[0], w_query[...], preferred_element_type=F32
            ).astype(BF16)
    normed = jnp.concatenate(normed, axis=0)
    pair_ref[:, :features] = jnp.dot(normed, w_key[...], preferred_element_type=F32).astype(BF16)
    pair_ref[:, features:] = jnp.dot(normed, w_value[...], preferred_element_type=F32).astype(BF16)


LANES = 128
CHUNK = 32
SLOTS = 2


def pair_scores(query_ref, pairs, at, score_ref):
    nodes = query_ref.shape[0]
    width = LANES // 2
    first = lax.broadcasted_iota(jnp.int32, (nodes, LANES), 1) < width
    query = query_ref[:, at].astype(F32) * width**-0.5
    query = jnp.concatenate(
        [jnp.where(first, query, 0.0).astype(BF16), jnp.where(first, 0.0, query).astype(BF16)], axis=0
    )
    start = 0
    for keys in pairs:
        count = keys.shape[0]
        score_ref[:, start : start + count] = lax.dot_general(
            query, keys[:, at], (((1,), (1,)), ((), ())), preferred_element_type=F32
        )
        start += count


def pair_weights(score_ref, bias_ref, weight_ref, floors):
    nodes = bias_ref.shape[0]
    peaks = []
    for start in range(0, 2 * nodes, CHUNK):
        rows = slice(start, start + CHUNK)
        there = slice(start % nodes, start % nodes + CHUNK)
        scores = score_ref[rows] + bias_ref[there]
        peak = jnp.max(scores, axis=1, keepdims=True)
        if floors is not None:
            peak = jnp.maximum(peak, floors[start // nodes][there])
        weight_ref[rows] = jnp.exp(scores - peak).astype(BF16)
        peaks.append(jnp.broadcast_to(peak, (CHUNK, LANES)))
    return jnp.concatenate(peaks, axis=0)


def pair_values(weight_ref, pairs, at):
    total, start = None, 0
    for values in pairs:
        count = values.shape[0]
        rhs = jnp.concatenate([values[:, at], jnp.ones((count, LANES), BF16)], axis=1)
        part = jnp.dot(weight_ref[:, start : start + count], rhs, preferred_element_type=F32)
        total = part if total is None else total + part
        start += count
    return total[:, :LANES], total[:, LANES:]


def attention(query_ref, pairs, bias_ref, score_ref, weight_ref, peak_ref, store):
    nodes, features = query_ref.shape
    width = LANES // 2
    first = lax.broadcasted_iota(jnp.int32, (nodes, LANES), 1) < width
    ats = [slice(base, base + LANES) for base in range(0, features, LANES)]
    slots = score_ref.shape[0]
    for pair in range(min(slots - 1, len(ats))):
        pair_scores(query_ref, pairs, ats[pair], score_ref.at[pair])
    for pair, at in enumerate(ats):
        ahead = pair + slots - 1
        if ahead < len(ats):
            pair_scores(query_ref, pairs, ats[ahead], score_ref.at[ahead % slots])
        floors = None
        if peak_ref is not None:
            old = peak_ref[:, at]
            floors = [old[:, :1], old[:, width : width + 1]]
        slot = pair % slots
        peaks = pair_weights(score_ref.at[slot], bias_ref, weight_ref.at[slot], floors)
        value_at = slice(at.start + features, at.stop + features)
        values, sums = pair_values(weight_ref.at[slot], pairs, value_at)
        store(at, *(jnp.where(first, a[:nodes], a[nodes:]) for a in (values, sums, peaks)))


def far_kernel(mean_ref, w_embed, w_encode, w_key, w_value, gain, *refs):
    feats, pair_ref = [feat.now() for feat in refs[:-1]], refs[-1]
    sector_rows(
        mean_ref, gain.now(), w_embed, w_encode, None, w_key, w_value, feats, None, None, pair_ref
    )


def own_kernel(
    count, mean_ref, bias_ref, w_embed, w_encode, w_query, w_key, w_value, gain, *refs
):
    feats, refs = [feat.now() for feat in refs[:count]], refs[count:]
    latent_ref, query_ref, pair_ref, mixed_ref, peak_ref, sum_ref, score_ref, weight_ref = refs
    nodes, features = query_ref.shape
    sector_rows(
        mean_ref, gain.now(), w_embed, w_encode, w_query, w_key, w_value, feats,
        latent_ref, query_ref, pair_ref,
    )

    def store(at, values, sums, peaks):
        mixed_ref[:, at] = values
        sum_ref[:, at] = sums
        peak_ref[:, at] = peaks

    attention(query_ref, [pair_ref], bias_ref, score_ref, weight_ref, None, store)


def attend_kernel(
    near_ref, far_ref, bias_ref, latent_ref, query_ref, mixed_ref, peak_ref, sum_ref,
    w_output, w_decode, gain_dec, w_read, out_ref, score_ref, weight_ref, context_ref,
):
    nodes, features = latent_ref.shape

    def store(at, values, sums, peaks):
        fade = jnp.exp(peak_ref[:, at] - peaks)
        values = values + fade * mixed_ref[:, at]
        context_ref[:, at] = (values / (sums + fade * sum_ref[:, at])).astype(BF16)

    attention(query_ref, [near_ref, far_ref], bias_ref, score_ref, weight_ref, peak_ref, store)
    mixed = latent_ref[...] + jnp.dot(context_ref[...], w_output[...], preferred_element_type=F32)
    normed_out = layer_norm(mixed, gain_dec.now()[...]).astype(BF16)
    decoded = silu(jnp.dot(normed_out, w_decode[...], preferred_element_type=F32)).astype(BF16)
    out_ref[...] = lax.dot_general(
        w_read.now()[...], decoded, (((1,), (1,)), ((), ())), preferred_element_type=F32
    ).astype(BF16)


def decode_kernel(bands, sectors, parts, dec, reads, base_ref, out_ref, wide=None, signals=None):
    dec_ref = dec.now()
    rows, cols = dec_ref.shape[1:]
    nodes = parts[0][1].stop - parts[0][1].start
    iota = lax.broadcasted_iota(jnp.int32, (nodes, 2 * cols), 0).astype(F32).astype(BF16)
    one = jnp.ones((nodes, 2 * cols), BF16)
    none = jnp.zeros((nodes, 2 * cols), BF16)
    block, member = place_of(dec_ref[...], nodes, bands, sectors)
    copies, half = [], rows // 2
    for row in range(0, rows, 2):
        at = slice(row * cols, (row + 2) * cols)
        update = None
        for (part, there), read_ref in zip(parts, reads):
            code = jnp.where(block == part, member, -1.0)
            code = jnp.concatenate([code[:, row], code[:, row + 1]], axis=1).astype(BF16)
            counts = none
            for slot in range(code.shape[0]):
                counts = counts + jnp.where(iota == code[slot : slot + 1], one, none)
            share = jnp.dot(read_ref[:, there], counts, preferred_element_type=F32)
            update = share if update is None else update + share
        update = base_ref[:, at].astype(F32) + update / 3.0
        if wide is None:
            out_ref[:, at] = update
            continue
        wide[:, row, :] = update[:, :cols]
        wide[:, row + 1, :] = update[:, cols:]
        if (row + 2) % half == 0:
            done = slice(row + 2 - half, row + 2)
            copies.append(
                pltpu.make_async_copy(
                    wide.at[:, done], out_ref.at[:, done], signals.at[len(copies)]
                )
            )
            copies[-1].start()
    for copy in copies:
        copy.wait()


class Late:
    def __init__(self, source, target, semaphore):
        self.target = target
        self.copy = pltpu.make_async_copy(source, target, semaphore)
        self.copy.start()
        self.waited = False

    def now(self):
        if not self.waited:
            self.copy.wait()
            self.waited = True
        return self.target


def call(name, kernel, outs, operands, late=(), scratch=(), mib=8, micros=1, out_memory=pltpu.VMEM):
    single = not isinstance(outs, (list, tuple))
    outs = [outs] if single else list(outs)
    n_in, n_late, n_out = len(operands), len(late), len(outs)

    def run(*refs):
        ins, refs = refs[:n_in], refs[n_in:]
        sources, refs = refs[:n_late], refs[n_late:]
        results, refs = refs[:n_out], refs[n_out:]
        targets, refs = refs[:n_late], refs[n_late:]
        if n_late:
            semaphores, refs = refs[0], refs[1:]
        fetched = [
            Late(source, target, semaphores.at[index])
            for index, (source, target) in enumerate(zip(sources, targets))
        ]
        kernel(*ins, *fetched, *results, *refs)

    fetch = [pltpu.VMEM(a.shape, a.dtype) for a in late]
    signals = [pltpu.SemaphoreType.DMA((n_late,))] if n_late else []
    specs = [whole()] * n_in + [whole(pltpu.HBM)] * n_late
    result = pl.pallas_call(
        run,
        name=name,
        out_shape=outs,
        in_specs=specs,
        out_specs=[whole(out_memory)] * n_out,
        scratch_shapes=fetch + signals + list(scratch),
        compiler_params=params(mib),
        cost_estimate=pl.CostEstimate(
            flops=int(micros * 5e8), bytes_accessed=int(micros * 3e6), transcendentals=0
        ),
    )(*operands, *late)
    return result[0] if single else result


def after(value, *earlier):
    return lax.optimization_barrier((value,) + earlier)[0]


def body(
    grid_state, mesh_feat, enc_src, enc_count, nbr_ids, nbr_count, dec_src,
    w_embed, w_encode, w_query, w_key, w_value, w_output, w_decode, w_readout, norm_attn, norm_dec,
):
    shape = jax.ShapeDtypeStruct
    bands, sectors = lax.axis_size("lat"), lax.axis_size("lon")
    variables, rows, cols = grid_state.shape
    nodes, features = mesh_feat.shape
    slots = enc_src.shape[0]
    cells, rim = rows * cols, rows * HALO
    sector_nodes = bands * nodes

    first = call("first", first_kernel, shape((8, LANES), F32), (), micros=20)
    near_rim, far_rim, live = call(
        "prep",
        prep_kernel,
        [
            shape((variables, rim), BF16),
            shape((variables, rim), BF16),
            shape((slots, nodes), jnp.int32),
        ],
        (first, grid_state, enc_src, enc_count[None]),
        scratch=[pltpu.VMEM((variables, rows, cols), F32)],
        micros=2,
    )
    feat = after(mesh_feat, live)
    far_rim = from_far(far_rim)
    near_rim = from_near(near_rim)
    feats = [mesh_feat] + from_bands(mesh_feat)
    lives = [live] + from_bands(live)
    flat = call(
        "flat",
        flat_kernel,
        shape((variables, cells), BF16),
        (after(grid_state, live),),
        scratch=[pltpu.VMEM((variables, rows, cols), F32)],
        micros=0.1,
    )
    encoded = []
    for step, source in enumerate(lives):
        encoded += call(
            "encode",
            encode_kernel,
            [shape((variables, nodes), F32), shape((2 * rim, nodes), BF16)],
                (source, flat),
            micros=0.1 if step else 3,
        )
    feat_far = from_far(feat)
    summed, sent = call(
        "rim",
        rim_kernel,
        [shape((variables, sector_nodes), F32), shape((variables, sector_nodes), BF16)],
        (near_rim, far_rim, *encoded), micros=0.1,
    )
    received = from_bands(sent)
    bias_own, bias_rest = call(
        "bias",
        functools.partial(bias_kernel, bands, sectors),
        [shape((nodes, sector_nodes), F32), shape((nodes, 2 * sector_nodes), F32)],
        (),
        late=(after(nbr_ids, summed), nbr_count[None]),
        micros=30,
    )
    mean = call(
        "mean",
        mean_kernel,
        shape((variables, sector_nodes), BF16),
        (after(summed, bias_own), *received, *lives),
        micros=0.1,
    )
    feats_far = [feat_far] + from_bands(after(feat_far, mean))
    mean_far = from_far(mean)
    latent, query, pair, mixed, peak, total = call(
        "own",
        functools.partial(own_kernel, len(feats)),
        [
            shape((nodes, features), F32),
            shape((nodes, features), BF16),
            shape((sector_nodes, 2 * features), BF16),
        ]
        + [shape((nodes, features), F32)] * 3,
        (mean, bias_own, after(w_embed, feat_far), w_encode, w_query, w_key, w_value),
        late=(norm_attn[None], *feats),
        scratch=[
            pltpu.VMEM((SLOTS, 2 * nodes, sector_nodes), F32),
            pltpu.VMEM((SLOTS, 2 * nodes, sector_nodes), BF16),
        ],
        mib=30,
        micros=10,
    )
    pair_near = from_near(pair)
    pair_far = call(
        "far",
        far_kernel,
        shape((sector_nodes, 2 * features), BF16),
        (mean_far, after(w_embed, pair), w_encode, w_key, w_value),
        late=(norm_attn[None], *feats_far),
        mib=16,
        micros=60,
    )
    readout = call(
        "attend",
        attend_kernel,
        shape((variables, nodes), BF16),
        (pair_near, pair_far, bias_rest, latent, query, mixed, peak, total, w_output, w_decode),
        late=(norm_dec[None], w_readout.T),
        scratch=[
            pltpu.VMEM((SLOTS, 2 * nodes, 2 * sector_nodes), F32),
            pltpu.VMEM((SLOTS, 2 * nodes, 2 * sector_nodes), BF16),
            pltpu.VMEM((nodes, features), BF16),
        ],
        mib=28,
        micros=12,
    )
    sums = shape((variables, cells), F32)
    decode = functools.partial(decode_kernel, bands, sectors)
    spots = [slice(band * nodes, (band + 1) * nodes) for band in range(bands)]
    own_sums = call(
        "decode_own",
        lambda read, base, dec, out: decode([(0, spots[0])], dec, [read], base, out),
        sums,
        (readout, flat),
        late=(dec_src,),
        micros=0.1,
    )
    reads = jnp.concatenate([readout] + from_bands(readout), axis=1)
    reads = after(reads, own_sums)
    read_far = from_far(reads)
    read_near = from_near(reads)
    near_sums = call(
        "decode_near",
        lambda base, own, near, dec, out: decode(
            list(enumerate(spots))[1:] + list(enumerate(spots, bands)),
            dec, [own] * (bands - 1) + [near] * bands, base, out,
        ),
        sums,
        (own_sums, reads, read_near),
        late=(dec_src,),
        micros=0.1,
    )
    return call(
        "decode_far",
        lambda base, far, dec, out, *more: decode(
            list(enumerate(spots, 2 * bands)), dec, [far] * bands, base, out, *more
        ),
        shape(grid_state.shape, F32),
        (near_sums, read_far),
        late=(dec_src,),
        scratch=[pltpu.VMEM(grid_state.shape, F32), pltpu.SemaphoreType.DMA((2,))],
        out_memory=pltpu.HBM,
        micros=0.1,
    )


def solution(mesh):
    in_specs = (
        P(None, "lat", "lon"),
        P(("lat", "lon"), None),
        P(None, ("lat", "lon")),
        P(("lat", "lon")),
        P(None, ("lat", "lon")),
        P(("lat", "lon")),
        P(None, "lat", "lon"),
    ) + (P(),) * 10
    out_specs = P(None, "lat", "lon")
    return jax.shard_map(body, mesh=mesh, in_specs=in_specs, out_specs=out_specs, check_vma=False)
```

```python
import functools

import jax
import jax.numpy as jnp
from jax import lax
from jax.experimental import pallas as pl
from jax.experimental.pallas import tpu as pltpu
from jax.sharding import PartitionSpec as P

HEADS = 16
HALO = 16
BF16 = jnp.bfloat16
F32 = jnp.float32
MIB = 1024 * 1024


def params(mib):
    return pltpu.CompilerParams(vmem_limit_bytes=mib * MIB)


def whole(memory=pltpu.VMEM):
    return pl.BlockSpec(memory_space=memory)


def silu(value):
    return 0.5 * value * (1.0 + jnp.tanh(0.5 * value))


def layer_norm(inputs_f, gain):
    centre = inputs_f - jnp.mean(inputs_f, axis=-1, keepdims=True)
    spread = jnp.mean(centre * centre, axis=-1, keepdims=True)
    return centre * lax.rsqrt(spread + 1e-05) * gain


def from_bands(value):
    count = lax.axis_size("lat")
    return [
        lax.ppermute(value, "lat", [(i, (i - step) % count) for i in range(count)])
        for step in range(1, count)
    ]


def from_near(value):
    count = lax.axis_size("lon")
    return lax.ppermute(value, "lon", [(i, i ^ 1) for i in range(count)])


def from_far(value):
    count = lax.axis_size("lon")
    return lax.ppermute(value, "lon", [(i, (i - 1 + 2 * (i % 2)) % count) for i in range(count)])


def quotient(value_f, divisor):
    return jnp.floor((value_f + 0.5) * (1.0 / divisor))


def first_kernel(out_ref):
    out_ref[...] = jnp.zeros(out_ref.shape, F32)


def prep_kernel(first_ref, grid_ref, src_ref, count_ref, near_ref, far_ref, live_ref, wide):
    slot = lax.broadcasted_iota(jnp.int32, live_ref.shape, 0)
    live_ref[...] = jnp.where(slot < count_ref[...], src_ref[...], -1)
    rows, cols = grid_ref.shape[1:]
    per_tile = cols // HALO
    odd = lax.axis_index("lon") % 2
    near_at = jnp.where(odd == 0, cols - HALO, 0)
    far_at = cols - HALO - near_at
    lane = lax.broadcasted_iota(jnp.int32, (grid_ref.shape[0], cols), 1) // HALO
    wide[...] = grid_ref[...].astype(F32)
    for tile in range(rows // per_tile):
        near, far = None, None
        for place in range(per_tile):
            line = wide[:, tile * per_tile + place, :]
            turned = [
                pltpu.roll(line, (place * HALO - start + cols) % cols, 1)
                for start in (near_at, far_at)
            ]
            near = turned[0] if near is None else jnp.where(lane == place, turned[0], near)
            far = turned[1] if far is None else jnp.where(lane == place, turned[1], far)
        near_ref[:, tile * cols : (tile + 1) * cols] = near.astype(BF16)
        far_ref[:, tile * cols : (tile + 1) * cols] = far.astype(BF16)


def flat_kernel(grid_ref, flat_ref, wide):
    rows, cols = grid_ref.shape[1:]
    wide[...] = grid_ref[...].astype(F32)
    for row in range(rows):
        flat_ref[:, row * cols : (row + 1) * cols] = wide[:, row, :].astype(BF16)


def encode_kernel(src_ref, flat_ref, out_ref, rim_ref):
    slots, nodes = src_ref.shape
    cells = flat_ref.shape[1]
    rim = rim_ref.shape[0] // 2
    rows = rim // HALO
    cols = cells // rows
    span = cols + 2 * HALO
    lanes = 128
    even = lax.axis_index("lon") % 2 == 0
    source = src_ref[...].astype(F32)
    row_of = quotient(source, span)
    col_of = source - row_of * span
    row_of = row_of - (lax.axis_index("lat") * rows).astype(F32)
    iota = lax.broadcasted_iota(jnp.int32, (span, lanes), 0).astype(F32).astype(BF16)
    one = jnp.ones((span, lanes), BF16)
    none = jnp.zeros((span, lanes), BF16)
    west = pl.multiple_of(jnp.where(even, rim, 0), rim)
    east = pl.multiple_of(jnp.where(even, 0, rim), rim)
    summed = None
    for row in range(0, rows, 2):
        parts = []
        for r in (row, row + 1):
            code = jnp.where(row_of == r, col_of, -1.0).astype(BF16)
            line = []
            for tile in range(nodes // lanes):
                at = slice(tile * lanes, (tile + 1) * lanes)
                total = none
                for slot in range(slots):
                    total = total + jnp.where(iota == code[slot : slot + 1, at], one, none)
                rim_ref[pl.ds(west + r * HALO, HALO), at] = total[:HALO]
                rim_ref[pl.ds(east + r * HALO, HALO), at] = total[HALO + cols :]
                line.append(total[HALO : HALO + cols])
            parts.append(jnp.concatenate(line, axis=1))
        part = slice(row * cols, (row + 2) * cols)
        got = jnp.dot(flat_ref[:, part], jnp.concatenate(parts, axis=0), preferred_element_type=F32)
        summed = got if summed is None else summed + got
    out_ref[...] = summed


def rim_kernel(near_ref, far_ref, *refs):
    out_ref, sent_ref = refs[-2:]
    rim = near_ref.shape[1]
    for part in range(len(refs) // 2 - 1):
        summed, counts = refs[2 * part], refs[2 * part + 1]
        nodes = summed.shape[1]
        total = summed[...]
        total += jnp.dot(near_ref[...], counts[:rim], preferred_element_type=F32)
        total += jnp.dot(far_ref[...], counts[rim:], preferred_element_type=F32)
        out_ref[:, part * nodes : (part + 1) * nodes] = total
    sent_ref[...] = out_ref[...].astype(BF16)


def mean_kernel(own_ref, *refs):
    out_ref = refs[-1]
    bands = len(refs) // 2
    others, sources = refs[: bands - 1], refs[bands - 1 : -1]
    nodes = own_ref.shape[1] // bands
    for band in range(bands):
        at = slice(band * nodes, (band + 1) * nodes)
        count = jnp.sum(jnp.where(sources[band][...] >= 0, 1.0, 0.0), axis=0, keepdims=True)
        total = own_ref[:, at]
        for step, other in enumerate(others, 1):
            there = (band - step) % bands
            total = total + other[:, there * nodes : (there + 1) * nodes].astype(F32)
        out_ref[:, at] = (total / count).astype(BF16)


def place_of(ids, node_count, bands, sectors):
    ids_f = ids.astype(F32)
    device = quotient(ids_f, node_count)
    member = ids_f - device * node_count
    band = quotient(device, sectors)
    sector = device - band * sectors
    mine = lax.axis_index("lon")
    near = mine + 1 - 2 * (mine % 2)
    side = jnp.where(sector == mine.astype(F32), 0.0, 2.0)
    side = jnp.where(sector == near.astype(F32), 1.0, side)
    band = band - lax.axis_index("lat").astype(F32)
    band = jnp.where(band < 0, band + bands, band)
    return side * bands + band, member


def bias_kernel(bands, sectors, ids, count, own_ref, rest_ref):
    ids_ref, count_ref = ids.now(), count.now()
    slots, nodes = ids_ref.shape
    lanes = 128
    block, member = place_of(ids_ref[...], nodes, bands, sectors)
    slot_of = lax.broadcasted_iota(jnp.int32, (slots, nodes), 0)
    block = jnp.where(slot_of < count_ref[...], block, -1.0)
    iota = lax.broadcasted_iota(jnp.int32, (nodes, lanes), 0).astype(F32).astype(BF16)
    shut = jnp.full((nodes, lanes), -1e30, BF16)
    opened = jnp.zeros((nodes, lanes), BF16)
    for part in range(3 * bands):
        code = jnp.where(block == part, member, -1.0).astype(BF16)
        ref, index = (own_ref, part) if part < bands else (rest_ref, part - bands)
        for tile in range(nodes // lanes):
            at = slice(tile * lanes, (tile + 1) * lanes)
            total = shut
            for slot in range(slots):
                total = jnp.where(iota == code[slot : slot + 1, at], opened, total)
            ref[at, index * nodes : (index + 1) * nodes] = total.astype(F32).T


def latent_of(mean, feat, w_embed, w_encode):
    embedded = silu(
        lax.dot_general(mean, w_embed, (((0,), (0,)), ((), ())), preferred_element_type=F32)
    ).astype(BF16)
    return feat.astype(F32) + jnp.dot(embedded, w_encode, preferred_element_type=F32)


def sector_rows(
    mean_ref, gain_ref, w_embed, w_encode, w_query, w_key, w_value, feats, latent_ref, query_ref, pair_ref
):
    features = feats[0].shape[1]
    normed, start = [], 0
    for part, feat in enumerate(feats):
        at = slice(start, start + feat.shape[0])
        start = at.stop
        latent = latent_of(mean_ref[:, at], feat[...], w_embed[...], w_encode[...])
        normed.append(layer_norm(latent, gain_ref[...]).astype(BF16))
        if part == 0 and latent_ref is not None:
            latent_ref[...] = latent
            query_ref[...] = jnp.dot(
                normed[0], w_query[...], preferred_element_type=F32
            ).astype(BF16)
    normed = jnp.concatenate(normed, axis=0)
    pair_ref[:, :features] = jnp.dot(normed, w_key[...], preferred_element_type=F32).astype(BF16)
    pair_ref[:, features:] = jnp.dot(normed, w_value[...], preferred_element_type=F32).astype(BF16)


LANES = 128
CHUNK = 32
SLOTS = 2


def pair_scores(query_ref, pairs, at, score_ref):
    nodes = query_ref.shape[0]
    width = LANES // 2
    first = lax.broadcasted_iota(jnp.int32, (nodes, LANES), 1) < width
    query = query_ref[:, at].astype(F32) * width**-0.5
    query = jnp.concatenate(
        [jnp.where(first, query, 0.0).astype(BF16), jnp.where(first, 0.0, query).astype(BF16)], axis=0
    )
    start = 0
    for keys in pairs:
        count = keys.shape[0]
        score_ref[:, start : start + count] = lax.dot_general(
            query, keys[:, at], (((1,), (1,)), ((), ())), preferred_element_type=F32
        )
        start += count


def pair_weights(score_ref, bias_ref, weight_ref, floors):
    nodes = bias_ref.shape[0]
    peaks = []
    for start in range(0, 2 * nodes, CHUNK):
        rows = slice(start, start + CHUNK)
        there = slice(start % nodes, start % nodes + CHUNK)
        scores = score_ref[rows] + bias_ref[there]
        peak = jnp.max(scores, axis=1, keepdims=True)
        if floors is not None:
            peak = jnp.maximum(peak, floors[start // nodes][there])
        weight_ref[rows] = jnp.exp(scores - peak).astype(BF16)
        peaks.append(jnp.broadcast_to(peak, (CHUNK, LANES)))
    return jnp.concatenate(peaks, axis=0)


def pair_values(weight_ref, pairs, at):
    total, start = None, 0
    for values in pairs:
        count = values.shape[0]
        rhs = jnp.concatenate([values[:, at], jnp.ones((count, LANES), BF16)], axis=1)
        part = jnp.dot(weight_ref[:, start : start + count], rhs, preferred_element_type=F32)
        total = part if total is None else total + part
        start += count
    return total[:, :LANES], total[:, LANES:]


def attention(query_ref, pairs, bias_ref, score_ref, weight_ref, peak_ref, store):
    nodes, features = query_ref.shape
    width = LANES // 2
    first = lax.broadcasted_iota(jnp.int32, (nodes, LANES), 1) < width
    ats = [slice(base, base + LANES) for base in range(0, features, LANES)]
    slots = score_ref.shape[0]
    for pair in range(min(slots - 1, len(ats))):
        pair_scores(query_ref, pairs, ats[pair], score_ref.at[pair])
    for pair, at in enumerate(ats):
        ahead = pair + slots - 1
        if ahead < len(ats):
            pair_scores(query_ref, pairs, ats[ahead], score_ref.at[ahead % slots])
        floors = None
        if peak_ref is not None:
            old = peak_ref[:, at]
            floors = [old[:, :1], old[:, width : width + 1]]
        slot = pair % slots
        peaks = pair_weights(score_ref.at[slot], bias_ref, weight_ref.at[slot], floors)
        value_at = slice(at.start + features, at.stop + features)
        values, sums = pair_values(weight_ref.at[slot], pairs, value_at)
        store(at, *(jnp.where(first, a[:nodes], a[nodes:]) for a in (values, sums, peaks)))


def far_kernel(at, mean_ref, w_embed, w_encode, w_key, w_value, gain, feat, pair_ref):
    sector_rows(
        mean_ref.at[:, at], gain.now(), w_embed, w_encode, None, w_key, w_value, [feat.now()],
        None, None, pair_ref,
    )


def own_kernel(
    count, mean_ref, bias_ref, w_embed, w_encode, w_query, w_key, w_value, gain, *refs
):
    feats, refs = [feat.now() for feat in refs[:count]], refs[count:]
    latent_ref, query_ref, pair_ref, mixed_ref, peak_ref, sum_ref, score_ref, weight_ref = refs
    nodes, features = query_ref.shape
    sector_rows(
        mean_ref, gain.now(), w_embed, w_encode, w_query, w_key, w_value, feats,
        latent_ref, query_ref, pair_ref,
    )

    def store(at, values, sums, peaks):
        mixed_ref[:, at] = values
        sum_ref[:, at] = sums
        peak_ref[:, at] = peaks

    attention(query_ref, [pair_ref], bias_ref, score_ref, weight_ref, None, store)


def attend_kernel(
    bands, near_ref, *refs
):
    attend_rows([near_ref, *refs[:bands]], *refs[bands:])


def attend_rows(
    pairs, bias_ref, latent_ref, query_ref, mixed_ref, peak_ref, sum_ref,
    w_output, w_decode, gain_dec, w_read, out_ref, score_ref, weight_ref, context_ref,
):
    nodes, features = latent_ref.shape

    def store(at, values, sums, peaks):
        fade = jnp.exp(peak_ref[:, at] - peaks)
        values = values + fade * mixed_ref[:, at]
        context_ref[:, at] = (values / (sums + fade * sum_ref[:, at])).astype(BF16)

    attention(query_ref, pairs, bias_ref, score_ref, weight_ref, peak_ref, store)
    mixed = latent_ref[...] + jnp.dot(context_ref[...], w_output[...], preferred_element_type=F32)
    normed_out = layer_norm(mixed, gain_dec.now()[...]).astype(BF16)
    decoded = silu(jnp.dot(normed_out, w_decode[...], preferred_element_type=F32)).astype(BF16)
    out_ref[...] = lax.dot_general(
        w_read.now()[...], decoded, (((1,), (1,)), ((), ())), preferred_element_type=F32
    ).astype(BF16)


def cell_counts(block, member, part, row, nodes):
    lanes = 2 * block.shape[2]
    iota = lax.broadcasted_iota(jnp.int32, (nodes, lanes), 0).astype(F32).astype(BF16)
    one, none = jnp.ones((nodes, lanes), BF16), jnp.zeros((nodes, lanes), BF16)
    code = jnp.where(block == part, member, -1.0)
    code = jnp.concatenate([code[:, row], code[:, row + 1]], axis=1).astype(BF16)
    counts = none
    for slot in range(code.shape[0]):
        counts = counts + jnp.where(iota == code[slot : slot + 1], one, none)
    return counts


def decode_kernel(bands, sectors, parts, later, dec, reads, base_ref, out_ref, *refs):
    dec_ref = dec.now()
    rows, cols = dec_ref.shape[1:]
    nodes = parts[0][1].stop - parts[0][1].start
    block, member = place_of(dec_ref[...], nodes, bands, sectors)
    for row in range(0, rows, 2):
        at = slice(row * cols, (row + 2) * cols)
        update = None
        for (part, there), read_ref in zip(parts, reads):
            counts = cell_counts(block, member, part, row, nodes)
            share = jnp.dot(read_ref[:, there], counts, preferred_element_type=F32)
            update = share if update is None else update + share
        out_ref[:, at] = base_ref[:, at].astype(F32) + update / 3.0
        for index, part in enumerate(later):
            refs[0][index * nodes : (index + 1) * nodes, at] = cell_counts(
                block, member, part, row, nodes
            )


def finish_kernel(base_ref, read_ref, counts_ref, out_ref, wide, signals):
    rows, cols = wide.shape[1:]
    copies, half = [], rows // 2
    for row in range(0, rows, 2):
        at = slice(row * cols, (row + 2) * cols)
        update = jnp.dot(read_ref[...], counts_ref[:, at], preferred_element_type=F32)
        update = base_ref[:, at] + update / 3.0
        wide[:, row, :] = update[:, :cols]
        wide[:, row + 1, :] = update[:, cols:]
        if (row + 2) % half == 0:
            done = slice(row + 2 - half, row + 2)
            copies.append(
                pltpu.make_async_copy(
                    wide.at[:, done], out_ref.at[:, done], signals.at[len(copies)]
                )
            )
            copies[-1].start()
    for copy in copies:
        copy.wait()


class Late:
    def __init__(self, source, target, semaphore):
        self.target = target
        self.copy = pltpu.make_async_copy(source, target, semaphore)
        self.copy.start()
        self.waited = False

    def now(self):
        if not self.waited:
            self.copy.wait()
            self.waited = True
        return self.target


def call(name, kernel, outs, operands, late=(), scratch=(), mib=8, micros=1, out_memory=pltpu.VMEM):
    single = not isinstance(outs, (list, tuple))
    outs = [outs] if single else list(outs)
    n_in, n_late, n_out = len(operands), len(late), len(outs)

    def run(*refs):
        ins, refs = refs[:n_in], refs[n_in:]
        sources, refs = refs[:n_late], refs[n_late:]
        results, refs = refs[:n_out], refs[n_out:]
        targets, refs = refs[:n_late], refs[n_late:]
        if n_late:
            semaphores, refs = refs[0], refs[1:]
        fetched = [
            Late(source, target, semaphores.at[index])
            for index, (source, target) in enumerate(zip(sources, targets))
        ]
        kernel(*ins, *fetched, *results, *refs)

    fetch = [pltpu.VMEM(a.shape, a.dtype) for a in late]
    signals = [pltpu.SemaphoreType.DMA((n_late,))] if n_late else []
    specs = [whole()] * n_in + [whole(pltpu.HBM)] * n_late
    result = pl.pallas_call(
        run,
        name=name,
        out_shape=outs,
        in_specs=specs,
        out_specs=[whole(out_memory)] * n_out,
        scratch_shapes=fetch + signals + list(scratch),
        compiler_params=params(mib),
        cost_estimate=pl.CostEstimate(
            flops=int(micros * 5e8), bytes_accessed=int(micros * 3e6), transcendentals=0
        ),
    )(*operands, *late)
    return result[0] if single else result


def after(value, *earlier):
    return lax.optimization_barrier((value,) + earlier)[0]


def body(
    grid_state, mesh_feat, enc_src, enc_count, nbr_ids, nbr_count, dec_src,
    w_embed, w_encode, w_query, w_key, w_value, w_output, w_decode, w_readout, norm_attn, norm_dec,
):
    shape = jax.ShapeDtypeStruct
    bands, sectors = lax.axis_size("lat"), lax.axis_size("lon")
    variables, rows, cols = grid_state.shape
    nodes, features = mesh_feat.shape
    slots = enc_src.shape[0]
    cells, rim = rows * cols, rows * HALO
    sector_nodes = bands * nodes

    first = call("first", first_kernel, shape((8, LANES), F32), (), micros=20)
    near_rim, far_rim, live = call(
        "prep",
        prep_kernel,
        [
            shape((variables, rim), BF16),
            shape((variables, rim), BF16),
            shape((slots, nodes), jnp.int32),
        ],
        (first, grid_state, enc_src, enc_count[None]),
        scratch=[pltpu.VMEM((variables, rows, cols), F32)],
        micros=2,
    )
    feat = after(mesh_feat, live)
    far_rim = from_far(far_rim)
    near_rim = from_near(near_rim)
    feats = [mesh_feat] + from_bands(mesh_feat)
    lives = [live] + from_bands(live)
    flat = call(
        "flat",
        flat_kernel,
        shape((variables, cells), BF16),
        (after(grid_state, live),),
        scratch=[pltpu.VMEM((variables, rows, cols), F32)],
        micros=0.1,
    )
    encoded = []
    for step, source in enumerate(lives):
        encoded += call(
            "encode",
            encode_kernel,
            [shape((variables, nodes), F32), shape((2 * rim, nodes), BF16)],
                (source, flat),
            micros=0.1 if step else 3,
        )
    feat_far = from_far(feat)
    summed, sent = call(
        "rim",
        rim_kernel,
        [shape((variables, sector_nodes), F32), shape((variables, sector_nodes), BF16)],
        (near_rim, far_rim, *encoded), micros=0.1,
    )
    received = from_bands(sent)
    bias_own, bias_rest = call(
        "bias",
        functools.partial(bias_kernel, bands, sectors),
        [shape((nodes, sector_nodes), F32), shape((nodes, 2 * sector_nodes), F32)],
        (),
        late=(after(nbr_ids, summed), nbr_count[None]),
        micros=30,
    )
    mean = call(
        "mean",
        mean_kernel,
        shape((variables, sector_nodes), BF16),
        (after(summed, bias_own), *received, *lives),
        micros=0.1,
    )
    feats_far = [feat_far] + from_bands(after(feat_far, mean))
    mean_far = from_far(mean)
    latent, query, pair, mixed, peak, total = call(
        "own",
        functools.partial(own_kernel, len(feats)),
        [
            shape((nodes, features), F32),
            shape((nodes, features), BF16),
            shape((sector_nodes, 2 * features), BF16),
        ]
        + [shape((nodes, features), F32)] * 3,
        (mean, bias_own, after(w_embed, feat_far), w_encode, w_query, w_key, w_value),
        late=(norm_attn[None], *feats),
        scratch=[
            pltpu.VMEM((SLOTS, 2 * nodes, sector_nodes), F32),
            pltpu.VMEM((SLOTS, 2 * nodes, sector_nodes), BF16),
        ],
        mib=30,
        micros=10,
    )
    pair_near = from_near(pair)
    pairs_far = []
    for band, source in enumerate(feats_far):
        at = slice(band * nodes, (band + 1) * nodes)
        pairs_far.append(
            call(
                "far",
                functools.partial(far_kernel, at),
                shape((nodes, 2 * features), BF16),
                (mean_far, after(w_embed, pair, *pairs_far), w_encode, w_key, w_value),
                late=(norm_attn[None], source),
                mib=16,
                micros=60 if band else 0.1,
            )
        )
    readout = call(
        "attend",
        functools.partial(attend_kernel, bands),
        shape((variables, nodes), BF16),
        (pair_near, *pairs_far, bias_rest, latent, query, mixed, peak, total, w_output, w_decode),
        late=(norm_dec[None], w_readout.T),
        scratch=[
            pltpu.VMEM((SLOTS, 2 * nodes, 2 * sector_nodes), F32),
            pltpu.VMEM((SLOTS, 2 * nodes, 2 * sector_nodes), BF16),
            pltpu.VMEM((nodes, features), BF16),
        ],
        mib=28,
        micros=12,
    )
    sums = shape((variables, cells), F32)
    decode = functools.partial(decode_kernel, bands, sectors)
    spots = [slice(band * nodes, (band + 1) * nodes) for band in range(bands)]
    own_sums = call(
        "decode_own",
        lambda read, base, dec, out: decode([(0, spots[0])], [], dec, [read], base, out),
        sums,
        (readout, flat),
        late=(dec_src,),
        micros=0.1,
    )
    reads = jnp.concatenate([readout] + from_bands(readout), axis=1)
    reads = after(reads, own_sums)
    read_far = from_far(reads)
    read_near = from_near(reads)
    far_blocks = [2 * bands + band for band in range(bands)]
    near_sums, far_counts = call(
        "decode_near",
        lambda base, own, near, dec, out, counts: decode(
            list(enumerate(spots))[1:] + list(enumerate(spots, bands)),
            far_blocks, dec, [own] * (bands - 1) + [near] * bands, base, out, counts,
        ),
        [sums, shape((sector_nodes, cells), BF16)],
        (own_sums, reads, read_near),
        late=(dec_src,),
        mib=12,
        micros=0.1,
    )
    return call(
        "finish",
        finish_kernel,
        shape(grid_state.shape, F32),
        (near_sums, read_far, far_counts),
        scratch=[pltpu.VMEM(grid_state.shape, F32), pltpu.SemaphoreType.DMA((2,))],
        out_memory=pltpu.HBM,
        micros=0.1,
    )


def solution(mesh):
    in_specs = (
        P(None, "lat", "lon"),
        P(("lat", "lon"), None),
        P(None, ("lat", "lon")),
        P(("lat", "lon")),
        P(None, ("lat", "lon")),
        P(("lat", "lon")),
        P(None, "lat", "lon"),
    ) + (P(),) * 10
    out_specs = P(None, "lat", "lon")
    return jax.shard_map(body, mesh=mesh, in_specs=in_specs, out_specs=out_specs, check_vma=False)
```

```python
import functools

import jax
import jax.numpy as jnp
from jax import lax
from jax.experimental import pallas as pl
from jax.experimental.pallas import tpu as pltpu
from jax.sharding import PartitionSpec as P

HEADS = 16
HALO = 16
BF16 = jnp.bfloat16
F32 = jnp.float32
MIB = 1024 * 1024


def params(mib):
    return pltpu.CompilerParams(vmem_limit_bytes=mib * MIB)


def whole(memory=pltpu.VMEM):
    return pl.BlockSpec(memory_space=memory)


def silu(value):
    return 0.5 * value * (1.0 + jnp.tanh(0.5 * value))


def layer_norm(inputs_f, gain):
    centre = inputs_f - jnp.mean(inputs_f, axis=-1, keepdims=True)
    spread = jnp.mean(centre * centre, axis=-1, keepdims=True)
    return centre * lax.rsqrt(spread + 1e-05) * gain


def from_bands(value):
    count = lax.axis_size("lat")
    return [
        lax.ppermute(value, "lat", [(i, (i - step) % count) for i in range(count)])
        for step in range(1, count)
    ]


def from_near(value):
    count = lax.axis_size("lon")
    return lax.ppermute(value, "lon", [(i, i ^ 1) for i in range(count)])


def from_far(value):
    count = lax.axis_size("lon")
    return lax.ppermute(value, "lon", [(i, (i - 1 + 2 * (i % 2)) % count) for i in range(count)])


def quotient(value_f, divisor):
    return jnp.floor((value_f + 0.5) * (1.0 / divisor))


def first_kernel(out_ref):
    out_ref[...] = jnp.zeros(out_ref.shape, F32)


def prep_kernel(first_ref, grid_ref, src_ref, count_ref, near_ref, far_ref, live_ref, wide):
    slot = lax.broadcasted_iota(jnp.int32, live_ref.shape, 0)
    live_ref[...] = jnp.where(slot < count_ref[...], src_ref[...], -1)
    rows, cols = grid_ref.shape[1:]
    per_tile = cols // HALO
    odd = lax.axis_index("lon") % 2
    near_at = jnp.where(odd == 0, cols - HALO, 0)
    far_at = cols - HALO - near_at
    lane = lax.broadcasted_iota(jnp.int32, (grid_ref.shape[0], cols), 1) // HALO
    wide[...] = grid_ref[...].astype(F32)
    for tile in range(rows // per_tile):
        near, far = None, None
        for place in range(per_tile):
            line = wide[:, tile * per_tile + place, :]
            turned = [
                pltpu.roll(line, (place * HALO - start + cols) % cols, 1)
                for start in (near_at, far_at)
            ]
            near = turned[0] if near is None else jnp.where(lane == place, turned[0], near)
            far = turned[1] if far is None else jnp.where(lane == place, turned[1], far)
        near_ref[:, tile * cols : (tile + 1) * cols] = near.astype(BF16)
        far_ref[:, tile * cols : (tile + 1) * cols] = far.astype(BF16)


def flat_kernel(grid_ref, flat_ref, wide):
    rows, cols = grid_ref.shape[1:]
    wide[...] = grid_ref[...].astype(F32)
    for row in range(rows):
        flat_ref[:, row * cols : (row + 1) * cols] = wide[:, row, :].astype(BF16)


def encode_kernel(src_ref, flat_ref, out_ref, rim_ref):
    slots, nodes = src_ref.shape
    cells = flat_ref.shape[1]
    rim = rim_ref.shape[0] // 2
    rows = rim // HALO
    cols = cells // rows
    span = cols + 2 * HALO
    lanes = 128
    even = lax.axis_index("lon") % 2 == 0
    source = src_ref[...].astype(F32)
    row_of = quotient(source, span)
    col_of = source - row_of * span
    row_of = row_of - (lax.axis_index("lat") * rows).astype(F32)
    iota = lax.broadcasted_iota(jnp.int32, (span, lanes), 0).astype(F32).astype(BF16)
    one = jnp.ones((span, lanes), BF16)
    none = jnp.zeros((span, lanes), BF16)
    west = pl.multiple_of(jnp.where(even, rim, 0), rim)
    east = pl.multiple_of(jnp.where(even, 0, rim), rim)
    summed = None
    for row in range(0, rows, 2):
        parts = []
        for r in (row, row + 1):
            code = jnp.where(row_of == r, col_of, -1.0).astype(BF16)
            line = []
            for tile in range(nodes // lanes):
                at = slice(tile * lanes, (tile + 1) * lanes)
                total = none
                for slot in range(slots):
                    total = total + jnp.where(iota == code[slot : slot + 1, at], one, none)
                rim_ref[pl.ds(west + r * HALO, HALO), at] = total[:HALO]
                rim_ref[pl.ds(east + r * HALO, HALO), at] = total[HALO + cols :]
                line.append(total[HALO : HALO + cols])
            parts.append(jnp.concatenate(line, axis=1))
        part = slice(row * cols, (row + 2) * cols)
        got = jnp.dot(flat_ref[:, part], jnp.concatenate(parts, axis=0), preferred_element_type=F32)
        summed = got if summed is None else summed + got
    out_ref[...] = summed


def rim_kernel(near_ref, far_ref, *refs):
    out_ref, sent_ref = refs[-2:]
    rim = near_ref.shape[1]
    for part in range(len(refs) // 2 - 1):
        summed, counts = refs[2 * part], refs[2 * part + 1]
        nodes = summed.shape[1]
        total = summed[...]
        total += jnp.dot(near_ref[...], counts[:rim], preferred_element_type=F32)
        total += jnp.dot(far_ref[...], counts[rim:], preferred_element_type=F32)
        out_ref[:, part * nodes : (part + 1) * nodes] = total
    sent_ref[...] = out_ref[...].astype(BF16)


def mean_kernel(own_ref, *refs):
    out_ref = refs[-1]
    bands = len(refs) // 2
    others, sources = refs[: bands - 1], refs[bands - 1 : -1]
    nodes = own_ref.shape[1] // bands
    for band in range(bands):
        at = slice(band * nodes, (band + 1) * nodes)
        count = jnp.sum(jnp.where(sources[band][...] >= 0, 1.0, 0.0), axis=0, keepdims=True)
        total = own_ref[:, at]
        for step, other in enumerate(others, 1):
            there = (band - step) % bands
            total = total + other[:, there * nodes : (there + 1) * nodes].astype(F32)
        out_ref[:, at] = (total / count).astype(BF16)


def place_of(ids, node_count, bands, sectors):
    ids_f = ids.astype(F32)
    device = quotient(ids_f, node_count)
    member = ids_f - device * node_count
    band = quotient(device, sectors)
    sector = device - band * sectors
    mine = lax.axis_index("lon")
    near = mine + 1 - 2 * (mine % 2)
    side = jnp.where(sector == mine.astype(F32), 0.0, 2.0)
    side = jnp.where(sector == near.astype(F32), 1.0, side)
    band = band - lax.axis_index("lat").astype(F32)
    band = jnp.where(band < 0, band + bands, band)
    return side * bands + band, member


def bias_kernel(bands, sectors, ids, count, own_ref, rest_ref):
    ids_ref, count_ref = ids.now(), count.now()
    slots, nodes = ids_ref.shape
    lanes = 128
    block, member = place_of(ids_ref[...], nodes, bands, sectors)
    slot_of = lax.broadcasted_iota(jnp.int32, (slots, nodes), 0)
    block = jnp.where(slot_of < count_ref[...], block, -1.0)
    iota = lax.broadcasted_iota(jnp.int32, (nodes, lanes), 0).astype(F32).astype(BF16)
    shut = jnp.full((nodes, lanes), -1e30, BF16)
    opened = jnp.zeros((nodes, lanes), BF16)
    for part in range(3 * bands):
        code = jnp.where(block == part, member, -1.0).astype(BF16)
        ref, index = (own_ref, part) if part < bands else (rest_ref, part - bands)
        for tile in range(nodes // lanes):
            at = slice(tile * lanes, (tile + 1) * lanes)
            total = shut
            for slot in range(slots):
                total = jnp.where(iota == code[slot : slot + 1, at], opened, total)
            ref[at, index * nodes : (index + 1) * nodes] = total.astype(F32).T


def latent_of(mean, feat, w_embed, w_encode):
    embedded = silu(
        lax.dot_general(mean, w_embed, (((0,), (0,)), ((), ())), preferred_element_type=F32)
    ).astype(BF16)
    return feat.astype(F32) + jnp.dot(embedded, w_encode, preferred_element_type=F32)


def sector_rows(
    mean_ref, gain_ref, w_embed, w_encode, w_query, w_key, w_value, feats, latent_ref, query_ref, pair_ref
):
    features = feats[0].shape[1]
    normed, start = [], 0
    for part, feat in enumerate(feats):
        at = slice(start, start + feat.shape[0])
        start = at.stop
        latent = latent_of(mean_ref[:, at], feat[...], w_embed[...], w_encode[...])
        normed.append(layer_norm(latent, gain_ref[...]).astype(BF16))
        if part == 0 and latent_ref is not None:
            latent_ref[...] = latent
            query_ref[...] = jnp.dot(
                normed[0], w_query[...], preferred_element_type=F32
            ).astype(BF16)
    normed = jnp.concatenate(normed, axis=0)
    pair_ref[:, :features] = jnp.dot(normed, w_key[...], preferred_element_type=F32).astype(BF16)
    pair_ref[:, features:] = jnp.dot(normed, w_value[...], preferred_element_type=F32).astype(BF16)


LANES = 128
CHUNK = 32
SLOTS = 2


def pair_scores(query_ref, pairs, at, score_ref):
    nodes = query_ref.shape[0]
    width = LANES // 2
    first = lax.broadcasted_iota(jnp.int32, (nodes, LANES), 1) < width
    query = query_ref[:, at].astype(F32) * width**-0.5
    query = jnp.concatenate(
        [jnp.where(first, query, 0.0).astype(BF16), jnp.where(first, 0.0, query).astype(BF16)], axis=0
    )
    start = 0
    for keys in pairs:
        count = keys.shape[0]
        score_ref[:, start : start + count] = lax.dot_general(
            query, keys[:, at], (((1,), (1,)), ((), ())), preferred_element_type=F32
        )
        start += count


def pair_weights(score_ref, bias_ref, weight_ref, floors):
    nodes = bias_ref.shape[0]
    peaks = []
    for start in range(0, 2 * nodes, CHUNK):
        rows = slice(start, start + CHUNK)
        there = slice(start % nodes, start % nodes + CHUNK)
        scores = score_ref[rows] + bias_ref[there]
        peak = jnp.max(scores, axis=1, keepdims=True)
        if floors is not None:
            peak = jnp.maximum(peak, floors[start // nodes][there])
        weight_ref[rows] = jnp.exp(scores - peak).astype(BF16)
        peaks.append(jnp.broadcast_to(peak, (CHUNK, LANES)))
    return jnp.concatenate(peaks, axis=0)


def pair_values(weight_ref, pairs, at):
    total, start = None, 0
    for values in pairs:
        count = values.shape[0]
        rhs = jnp.concatenate([values[:, at], jnp.ones((count, LANES), BF16)], axis=1)
        part = jnp.dot(weight_ref[:, start : start + count], rhs, preferred_element_type=F32)
        total = part if total is None else total + part
        start += count
    return total[:, :LANES], total[:, LANES:]


def attention(query_ref, pairs, bias_ref, score_ref, weight_ref, peak_ref, store):
    nodes, features = query_ref.shape
    width = LANES // 2
    first = lax.broadcasted_iota(jnp.int32, (nodes, LANES), 1) < width
    ats = [slice(base, base + LANES) for base in range(0, features, LANES)]
    slots = score_ref.shape[0]
    for pair in range(min(slots - 1, len(ats))):
        pair_scores(query_ref, pairs, ats[pair], score_ref.at[pair])
    for pair, at in enumerate(ats):
        ahead = pair + slots - 1
        if ahead < len(ats):
            pair_scores(query_ref, pairs, ats[ahead], score_ref.at[ahead % slots])
        floors = None
        if peak_ref is not None:
            old = peak_ref[:, at]
            floors = [old[:, :1], old[:, width : width + 1]]
        slot = pair % slots
        peaks = pair_weights(score_ref.at[slot], bias_ref, weight_ref.at[slot], floors)
        value_at = slice(at.start + features, at.stop + features)
        values, sums = pair_values(weight_ref.at[slot], pairs, value_at)
        store(at, *(jnp.where(first, a[:nodes], a[nodes:]) for a in (values, sums, peaks)))


def far_kernel(at, mean_ref, w_embed, w_encode, w_key, w_value, gain, feat, pair_ref):
    sector_rows(
        mean_ref.at[:, at], gain.now(), w_embed, w_encode, None, w_key, w_value, [feat.now()],
        None, None, pair_ref,
    )


def own_kernel(
    count, mean_ref, bias_ref, w_embed, w_encode, w_query, w_key, w_value, gain, *refs
):
    feats, refs = [feat.now() for feat in refs[:count]], refs[count:]
    latent_ref, query_ref, pair_ref, mixed_ref, peak_ref, sum_ref, score_ref, weight_ref = refs
    nodes, features = query_ref.shape
    sector_rows(
        mean_ref, gain.now(), w_embed, w_encode, w_query, w_key, w_value, feats,
        latent_ref, query_ref, pair_ref,
    )

    def store(at, values, sums, peaks):
        mixed_ref[:, at] = values
        sum_ref[:, at] = sums
        peak_ref[:, at] = peaks

    attention(query_ref, [pair_ref], bias_ref, score_ref, weight_ref, None, store)


def attend_kernel(
    bands, near_ref, *refs
):
    attend_rows([near_ref, *refs[:bands]], *refs[bands:])


def attend_rows(
    pairs, bias_ref, latent_ref, query_ref, mixed_ref, peak_ref, sum_ref,
    w_output, w_decode, gain_dec, w_read, out_ref, score_ref, weight_ref, context_ref,
):
    nodes, features = latent_ref.shape

    def store(at, values, sums, peaks):
        fade = jnp.exp(peak_ref[:, at] - peaks)
        values = values + fade * mixed_ref[:, at]
        context_ref[:, at] = (values / (sums + fade * sum_ref[:, at])).astype(BF16)

    attention(query_ref, pairs, bias_ref, score_ref, weight_ref, peak_ref, store)
    mixed = latent_ref[...] + jnp.dot(context_ref[...], w_output[...], preferred_element_type=F32)
    normed_out = layer_norm(mixed, gain_dec.now()[...]).astype(BF16)
    decoded = silu(jnp.dot(normed_out, w_decode[...], preferred_element_type=F32)).astype(BF16)
    out_ref[...] = lax.dot_general(
        w_read.now()[...], decoded, (((1,), (1,)), ((), ())), preferred_element_type=F32
    ).astype(BF16)


def cell_counts(block, member, part, row, nodes):
    lanes = 2 * block.shape[2]
    iota = lax.broadcasted_iota(jnp.int32, (nodes, lanes), 0).astype(F32).astype(BF16)
    one, none = jnp.ones((nodes, lanes), BF16), jnp.zeros((nodes, lanes), BF16)
    code = jnp.where(block == part, member, -1.0)
    code = jnp.concatenate([code[:, row], code[:, row + 1]], axis=1).astype(BF16)
    counts = none
    for slot in range(code.shape[0]):
        counts = counts + jnp.where(iota == code[slot : slot + 1], one, none)
    return counts


def decode_kernel(bands, sectors, parts, later, dec, reads, base_ref, out_ref, *refs):
    dec_ref = dec.now()
    rows, cols = dec_ref.shape[1:]
    nodes = parts[0][1].stop - parts[0][1].start
    block, member = place_of(dec_ref[...], nodes, bands, sectors)
    for row in range(0, rows, 2):
        at = slice(row * cols, (row + 2) * cols)
        update = None
        for (part, there), read_ref in zip(parts, reads):
            counts = cell_counts(block, member, part, row, nodes)
            share = jnp.dot(read_ref[:, there], counts, preferred_element_type=F32)
            update = share if update is None else update + share
        out_ref[:, at] = base_ref[:, at].astype(F32) + update / 3.0
        for index, part in enumerate(later):
            refs[0][index * nodes : (index + 1) * nodes, at] = cell_counts(
                block, member, part, row, nodes
            )


def finish_kernel(base_ref, read_ref, counts_ref, out_ref, wide, signals):
    rows, cols = wide.shape[1:]
    copies, half = [], rows // 2
    for row in range(0, rows, 2):
        at = slice(row * cols, (row + 2) * cols)
        update = jnp.dot(read_ref[...], counts_ref[:, at], preferred_element_type=F32)
        update = base_ref[:, at] + update / 3.0
        wide[:, row, :] = update[:, :cols]
        wide[:, row + 1, :] = update[:, cols:]
        if (row + 2) % half == 0:
            done = slice(row + 2 - half, row + 2)
            copies.append(
                pltpu.make_async_copy(
                    wide.at[:, done], out_ref.at[:, done], signals.at[len(copies)]
                )
            )
            copies[-1].start()
    for copy in copies:
        copy.wait()


class Late:
    def __init__(self, source, target, semaphore):
        self.target = target
        self.copy = pltpu.make_async_copy(source, target, semaphore)
        self.copy.start()
        self.waited = False

    def now(self):
        if not self.waited:
            self.copy.wait()
            self.waited = True
        return self.target


def call(name, kernel, outs, operands, late=(), scratch=(), mib=8, micros=1, out_memory=pltpu.VMEM):
    single = not isinstance(outs, (list, tuple))
    outs = [outs] if single else list(outs)
    n_in, n_late, n_out = len(operands), len(late), len(outs)

    def run(*refs):
        ins, refs = refs[:n_in], refs[n_in:]
        sources, refs = refs[:n_late], refs[n_late:]
        results, refs = refs[:n_out], refs[n_out:]
        targets, refs = refs[:n_late], refs[n_late:]
        if n_late:
            semaphores, refs = refs[0], refs[1:]
        fetched = [
            Late(source, target, semaphores.at[index])
            for index, (source, target) in enumerate(zip(sources, targets))
        ]
        kernel(*ins, *fetched, *results, *refs)

    fetch = [pltpu.VMEM(a.shape, a.dtype) for a in late]
    signals = [pltpu.SemaphoreType.DMA((n_late,))] if n_late else []
    specs = [whole()] * n_in + [whole(pltpu.HBM)] * n_late
    result = pl.pallas_call(
        run,
        name=name,
        out_shape=outs,
        in_specs=specs,
        out_specs=[whole(out_memory)] * n_out,
        scratch_shapes=fetch + signals + list(scratch),
        compiler_params=params(mib),
        cost_estimate=pl.CostEstimate(
            flops=int(micros * 5e8), bytes_accessed=int(micros * 3e6), transcendentals=0
        ),
    )(*operands, *late)
    return result[0] if single else result


def after(value, *earlier):
    return lax.optimization_barrier((value,) + earlier)[0]


def body(
    grid_state, mesh_feat, enc_src, enc_count, nbr_ids, nbr_count, dec_src,
    w_embed, w_encode, w_query, w_key, w_value, w_output, w_decode, w_readout, norm_attn, norm_dec,
):
    shape = jax.ShapeDtypeStruct
    bands, sectors = lax.axis_size("lat"), lax.axis_size("lon")
    variables, rows, cols = grid_state.shape
    nodes, features = mesh_feat.shape
    slots = enc_src.shape[0]
    cells, rim = rows * cols, rows * HALO
    sector_nodes = bands * nodes

    first = call("first", first_kernel, shape((8, LANES), F32), (), micros=20)
    near_rim, far_rim, live = call(
        "prep",
        prep_kernel,
        [
            shape((variables, rim), BF16),
            shape((variables, rim), BF16),
            shape((slots, nodes), jnp.int32),
        ],
        (first, grid_state, enc_src, enc_count[None]),
        scratch=[pltpu.VMEM((variables, rows, cols), F32)],
        micros=2,
    )
    feat = after(mesh_feat, live)
    far_rim = from_far(far_rim)
    near_rim = from_near(near_rim)
    feats = [mesh_feat] + from_bands(mesh_feat)
    lives = [live] + from_bands(live)
    flat = call(
        "flat",
        flat_kernel,
        shape((variables, cells), BF16),
        (after(grid_state, live),),
        scratch=[pltpu.VMEM((variables, rows, cols), F32)],
        micros=0.1,
    )
    encoded = []
    for step, source in enumerate(lives):
        encoded += call(
            "encode",
            encode_kernel,
            [shape((variables, nodes), F32), shape((2 * rim, nodes), BF16)],
                (source, flat),
            micros=0.1 if step else 3,
        )
    feat_far = from_far(feat)
    summed, sent = call(
        "rim",
        rim_kernel,
        [shape((variables, sector_nodes), F32), shape((variables, sector_nodes), BF16)],
        (near_rim, far_rim, *encoded), micros=0.1,
    )
    received = from_bands(sent)
    bias_own, bias_rest = call(
        "bias",
        functools.partial(bias_kernel, bands, sectors),
        [shape((nodes, sector_nodes), F32), shape((nodes, 2 * sector_nodes), F32)],
        (),
        late=(after(nbr_ids, summed), nbr_count[None]),
        micros=30,
    )
    mean = call(
        "mean",
        mean_kernel,
        shape((variables, sector_nodes), BF16),
        (after(summed, bias_own), *received, *lives),
        micros=0.1,
    )
    feats_far = [feat_far] + from_bands(after(feat_far, mean))
    mean_far = from_far(mean)
    latent, query, pair, mixed, peak, total = call(
        "own",
        functools.partial(own_kernel, len(feats)),
        [
            shape((nodes, features), F32),
            shape((nodes, features), BF16),
            shape((sector_nodes, 2 * features), BF16),
        ]
        + [shape((nodes, features), F32)] * 3,
        (mean, bias_own, after(w_embed, feat_far), w_encode, w_query, w_key, w_value),
        late=(norm_attn[None], *feats),
        scratch=[
            pltpu.VMEM((SLOTS, 2 * nodes, sector_nodes), F32),
            pltpu.VMEM((SLOTS, 2 * nodes, sector_nodes), BF16),
        ],
        mib=30,
        micros=10,
    )
    pair_near = from_near(pair)
    pairs_far = []
    for band, source in enumerate(feats_far):
        at = slice(band * nodes, (band + 1) * nodes)
        pairs_far.append(
            call(
                "far",
                functools.partial(far_kernel, at),
                shape((nodes, 2 * features), BF16),
                (mean_far, after(w_embed, pair, *pairs_far), w_encode, w_key, w_value),
                late=(norm_attn[None], source),
                mib=16,
                micros=60 if band else 0.1,
            )
        )
    readout = call(
        "attend",
        functools.partial(attend_kernel, bands),
        shape((variables, nodes), BF16),
        (pair_near, *pairs_far, bias_rest, latent, query, mixed, peak, total, w_output, w_decode),
        late=(norm_dec[None], w_readout.T),
        scratch=[
            pltpu.VMEM((SLOTS, 2 * nodes, 2 * sector_nodes), F32),
            pltpu.VMEM((SLOTS, 2 * nodes, 2 * sector_nodes), BF16),
            pltpu.VMEM((nodes, features), BF16),
        ],
        mib=40,
        micros=12,
    )
    sums = shape((variables, cells), F32)
    decode = functools.partial(decode_kernel, bands, sectors)
    spots = [slice(band * nodes, (band + 1) * nodes) for band in range(bands)]
    own_sums = call(
        "decode_own",
        lambda read, base, dec, out: decode([(0, spots[0])], [], dec, [read], base, out),
        sums,
        (readout, flat),
        late=(dec_src,),
        micros=0.1,
    )
    reads = jnp.concatenate([readout] + from_bands(readout), axis=1)
    reads = after(reads, own_sums)
    read_far = from_far(reads)
    read_near = from_near(reads)
    far_blocks = [2 * bands + band for band in range(bands)]
    near_sums, far_counts = call(
        "decode_near",
        lambda base, own, near, dec, out, counts: decode(
            list(enumerate(spots))[1:] + list(enumerate(spots, bands)),
            far_blocks, dec, [own] * (bands - 1) + [near] * bands, base, out, counts,
        ),
        [sums, shape((sector_nodes, cells), BF16)],
        (own_sums, reads, read_near),
        late=(dec_src,),
        mib=12,
        micros=0.1,
    )
    return call(
        "finish",
        finish_kernel,
        shape(grid_state.shape, F32),
        (near_sums, read_far, far_counts),
        scratch=[pltpu.VMEM(grid_state.shape, F32), pltpu.SemaphoreType.DMA((2,))],
        out_memory=pltpu.HBM,
        micros=0.1,
    )


def solution(mesh):
    in_specs = (
        P(None, "lat", "lon"),
        P(("lat", "lon"), None),
        P(None, ("lat", "lon")),
        P(("lat", "lon")),
        P(None, ("lat", "lon")),
        P(("lat", "lon")),
        P(None, "lat", "lon"),
    ) + (P(),) * 10
    out_specs = P(None, "lat", "lon")
    return jax.shard_map(body, mesh=mesh, in_specs=in_specs, out_specs=out_specs, check_vma=False)
```

```python
import functools

import jax
import jax.numpy as jnp
from jax import lax
from jax.experimental import pallas as pl
from jax.experimental.pallas import tpu as pltpu
from jax.sharding import PartitionSpec as P

HEADS = 16
HALO = 16
BF16 = jnp.bfloat16
F32 = jnp.float32
MIB = 1024 * 1024


def params(mib):
    return pltpu.CompilerParams(vmem_limit_bytes=mib * MIB)


def whole(memory=pltpu.VMEM):
    return pl.BlockSpec(memory_space=memory)


def silu(value):
    return 0.5 * value * (1.0 + jnp.tanh(0.5 * value))


def layer_norm(inputs_f, gain):
    centre = inputs_f - jnp.mean(inputs_f, axis=-1, keepdims=True)
    spread = jnp.mean(centre * centre, axis=-1, keepdims=True)
    return centre * lax.rsqrt(spread + 1e-05) * gain


def from_bands(value):
    count = lax.axis_size("lat")
    return [
        lax.ppermute(value, "lat", [(i, (i - step) % count) for i in range(count)])
        for step in range(1, count)
    ]


def from_near(value):
    count = lax.axis_size("lon")
    return lax.ppermute(value, "lon", [(i, i ^ 1) for i in range(count)])


def from_far(value):
    count = lax.axis_size("lon")
    return lax.ppermute(value, "lon", [(i, (i - 1 + 2 * (i % 2)) % count) for i in range(count)])


def quotient(value_f, divisor):
    return jnp.floor((value_f + 0.5) * (1.0 / divisor))


def first_kernel(out_ref):
    out_ref[...] = jnp.zeros(out_ref.shape, F32)


def prep_kernel(first_ref, grid_ref, src_ref, count_ref, near_ref, far_ref, live_ref, wide):
    slot = lax.broadcasted_iota(jnp.int32, live_ref.shape, 0)
    live_ref[...] = jnp.where(slot < count_ref[...], src_ref[...], -1)
    rows, cols = grid_ref.shape[1:]
    per_tile = cols // HALO
    odd = lax.axis_index("lon") % 2
    near_at = jnp.where(odd == 0, cols - HALO, 0)
    far_at = cols - HALO - near_at
    lane = lax.broadcasted_iota(jnp.int32, (grid_ref.shape[0], cols), 1) // HALO
    wide[...] = grid_ref[...].astype(F32)
    for tile in range(rows // per_tile):
        near, far = None, None
        for place in range(per_tile):
            line = wide[:, tile * per_tile + place, :]
            turned = [
                pltpu.roll(line, (place * HALO - start + cols) % cols, 1)
                for start in (near_at, far_at)
            ]
            near = turned[0] if near is None else jnp.where(lane == place, turned[0], near)
            far = turned[1] if far is None else jnp.where(lane == place, turned[1], far)
        near_ref[:, tile * cols : (tile + 1) * cols] = near.astype(BF16)
        far_ref[:, tile * cols : (tile + 1) * cols] = far.astype(BF16)


def flat_kernel(grid_ref, flat_ref, wide):
    rows, cols = grid_ref.shape[1:]
    wide[...] = grid_ref[...].astype(F32)
    for row in range(rows):
        flat_ref[:, row * cols : (row + 1) * cols] = wide[:, row, :].astype(BF16)


def encode_kernel(src_ref, flat_ref, out_ref, rim_ref):
    slots, nodes = src_ref.shape
    cells = flat_ref.shape[1]
    rim = rim_ref.shape[0] // 2
    rows = rim // HALO
    cols = cells // rows
    span = cols + 2 * HALO
    lanes = 128
    even = lax.axis_index("lon") % 2 == 0
    source = src_ref[...].astype(F32)
    row_of = quotient(source, span)
    col_of = source - row_of * span
    row_of = row_of - (lax.axis_index("lat") * rows).astype(F32)
    iota = lax.broadcasted_iota(jnp.int32, (span, lanes), 0).astype(F32).astype(BF16)
    one = jnp.ones((span, lanes), BF16)
    none = jnp.zeros((span, lanes), BF16)
    west = pl.multiple_of(jnp.where(even, rim, 0), rim)
    east = pl.multiple_of(jnp.where(even, 0, rim), rim)
    summed = None
    for row in range(0, rows, 2):
        parts = []
        for r in (row, row + 1):
            code = jnp.where(row_of == r, col_of, -1.0).astype(BF16)
            line = []
            for tile in range(nodes // lanes):
                at = slice(tile * lanes, (tile + 1) * lanes)
                total = none
                for slot in range(slots):
                    total = total + jnp.where(iota == code[slot : slot + 1, at], one, none)
                rim_ref[pl.ds(west + r * HALO, HALO), at] = total[:HALO]
                rim_ref[pl.ds(east + r * HALO, HALO), at] = total[HALO + cols :]
                line.append(total[HALO : HALO + cols])
            parts.append(jnp.concatenate(line, axis=1))
        part = slice(row * cols, (row + 2) * cols)
        got = jnp.dot(flat_ref[:, part], jnp.concatenate(parts, axis=0), preferred_element_type=F32)
        summed = got if summed is None else summed + got
    out_ref[...] = summed


def rim_kernel(near_ref, far_ref, *refs):
    out_ref, sent_ref = refs[-2:]
    rim = near_ref.shape[1]
    for part in range(len(refs) // 2 - 1):
        summed, counts = refs[2 * part], refs[2 * part + 1]
        nodes = summed.shape[1]
        total = summed[...]
        total += jnp.dot(near_ref[...], counts[:rim], preferred_element_type=F32)
        total += jnp.dot(far_ref[...], counts[rim:], preferred_element_type=F32)
        out_ref[:, part * nodes : (part + 1) * nodes] = total
    sent_ref[...] = out_ref[...].astype(BF16)


def mean_kernel(own_ref, *refs):
    out_ref = refs[-1]
    bands = len(refs) // 2
    others, sources = refs[: bands - 1], refs[bands - 1 : -1]
    nodes = own_ref.shape[1] // bands
    for band in range(bands):
        at = slice(band * nodes, (band + 1) * nodes)
        count = jnp.sum(jnp.where(sources[band][...] >= 0, 1.0, 0.0), axis=0, keepdims=True)
        total = own_ref[:, at]
        for step, other in enumerate(others, 1):
            there = (band - step) % bands
            total = total + other[:, there * nodes : (there + 1) * nodes].astype(F32)
        out_ref[:, at] = (total / count).astype(BF16)


def place_of(ids, node_count, bands, sectors):
    ids_f = ids.astype(F32)
    device = quotient(ids_f, node_count)
    member = ids_f - device * node_count
    band = quotient(device, sectors)
    sector = device - band * sectors
    mine = lax.axis_index("lon")
    near = mine + 1 - 2 * (mine % 2)
    side = jnp.where(sector == mine.astype(F32), 0.0, 2.0)
    side = jnp.where(sector == near.astype(F32), 1.0, side)
    band = band - lax.axis_index("lat").astype(F32)
    band = jnp.where(band < 0, band + bands, band)
    return side * bands + band, member


def bias_kernel(bands, sectors, ids, count, own_ref, rest_ref):
    ids_ref, count_ref = ids.now(), count.now()
    slots, nodes = ids_ref.shape
    lanes = 128
    block, member = place_of(ids_ref[...], nodes, bands, sectors)
    slot_of = lax.broadcasted_iota(jnp.int32, (slots, nodes), 0)
    block = jnp.where(slot_of < count_ref[...], block, -1.0)
    iota = lax.broadcasted_iota(jnp.int32, (nodes, lanes), 0).astype(F32).astype(BF16)
    shut = jnp.full((nodes, lanes), -1e30, BF16)
    opened = jnp.zeros((nodes, lanes), BF16)
    for part in range(3 * bands):
        code = jnp.where(block == part, member, -1.0).astype(BF16)
        ref, index = (own_ref, part) if part < bands else (rest_ref, part - bands)
        for tile in range(nodes // lanes):
            at = slice(tile * lanes, (tile + 1) * lanes)
            total = shut
            for slot in range(slots):
                total = jnp.where(iota == code[slot : slot + 1, at], opened, total)
            ref[at, index * nodes : (index + 1) * nodes] = total.astype(F32).T


def latent_of(mean, feat, w_embed, w_encode):
    embedded = silu(
        lax.dot_general(mean, w_embed, (((0,), (0,)), ((), ())), preferred_element_type=F32)
    ).astype(BF16)
    return feat.astype(F32) + jnp.dot(embedded, w_encode, preferred_element_type=F32)


def sector_rows(
    mean_ref, gain_ref, w_embed, w_encode, w_query, w_key, w_value, feats, latent_ref, query_ref, pair_ref
):
    features = feats[0].shape[1]
    normed, start = [], 0
    for part, feat in enumerate(feats):
        at = slice(start, start + feat.shape[0])
        start = at.stop
        latent = latent_of(mean_ref[:, at], feat[...], w_embed[...], w_encode[...])
        normed.append(layer_norm(latent, gain_ref[...]).astype(BF16))
        if part == 0 and latent_ref is not None:
            latent_ref[...] = latent
            query_ref[...] = jnp.dot(
                normed[0], w_query[...], preferred_element_type=F32
            ).astype(BF16)
    normed = jnp.concatenate(normed, axis=0)
    pair_ref[:, :features] = jnp.dot(normed, w_key[...], preferred_element_type=F32).astype(BF16)
    pair_ref[:, features:] = jnp.dot(normed, w_value[...], preferred_element_type=F32).astype(BF16)


LANES = 128
CHUNK = 32
SLOTS = 2


def pair_scores(query_ref, pairs, at, score_ref):
    nodes = query_ref.shape[0]
    width = LANES // 2
    first = lax.broadcasted_iota(jnp.int32, (nodes, LANES), 1) < width
    query = query_ref[:, at].astype(F32) * width**-0.5
    query = jnp.concatenate(
        [jnp.where(first, query, 0.0).astype(BF16), jnp.where(first, 0.0, query).astype(BF16)], axis=0
    )
    start = 0
    for keys in pairs:
        count = keys.shape[0]
        score_ref[:, start : start + count] = lax.dot_general(
            query, keys[:, at], (((1,), (1,)), ((), ())), preferred_element_type=F32
        )
        start += count


def pair_weights(score_ref, bias_ref, weight_ref, floors):
    nodes = bias_ref.shape[0]
    peaks = []
    for start in range(0, 2 * nodes, CHUNK):
        rows = slice(start, start + CHUNK)
        there = slice(start % nodes, start % nodes + CHUNK)
        scores = score_ref[rows] + bias_ref[there]
        peak = jnp.max(scores, axis=1, keepdims=True)
        if floors is not None:
            peak = jnp.maximum(peak, floors[start // nodes][there])
        weight_ref[rows] = jnp.exp(scores - peak).astype(BF16)
        peaks.append(jnp.broadcast_to(peak, (CHUNK, LANES)))
    return jnp.concatenate(peaks, axis=0)


def pair_values(weight_ref, pairs, at):
    total, start = None, 0
    for values in pairs:
        count = values.shape[0]
        rhs = jnp.concatenate([values[:, at], jnp.ones((count, LANES), BF16)], axis=1)
        part = jnp.dot(weight_ref[:, start : start + count], rhs, preferred_element_type=F32)
        total = part if total is None else total + part
        start += count
    return total[:, :LANES], total[:, LANES:]


def attention(query_ref, pairs, bias_ref, score_ref, weight_ref, peak_ref, store):
    nodes, features = query_ref.shape
    width = LANES // 2
    first = lax.broadcasted_iota(jnp.int32, (nodes, LANES), 1) < width
    ats = [slice(base, base + LANES) for base in range(0, features, LANES)]
    slots = score_ref.shape[0]
    for pair in range(min(slots - 1, len(ats))):
        pair_scores(query_ref, pairs, ats[pair], score_ref.at[pair])
    for pair, at in enumerate(ats):
        ahead = pair + slots - 1
        if ahead < len(ats):
            pair_scores(query_ref, pairs, ats[ahead], score_ref.at[ahead % slots])
        floors = None
        if peak_ref is not None:
            old = peak_ref[:, at]
            floors = [old[:, :1], old[:, width : width + 1]]
        slot = pair % slots
        peaks = pair_weights(score_ref.at[slot], bias_ref, weight_ref.at[slot], floors)
        value_at = slice(at.start + features, at.stop + features)
        values, sums = pair_values(weight_ref.at[slot], pairs, value_at)
        store(at, *(jnp.where(first, a[:nodes], a[nodes:]) for a in (values, sums, peaks)))


def far_kernel(at, mean_ref, w_embed, w_encode, w_key, w_value, gain, feat, pair_ref):
    sector_rows(
        mean_ref.at[:, at], gain.now(), w_embed, w_encode, None, w_key, w_value, [feat.now()],
        None, None, pair_ref,
    )


def own_kernel(
    count, mean_ref, bias_ref, w_embed, w_encode, w_query, w_key, w_value, gain, *refs
):
    feats, refs = [feat.now() for feat in refs[:count]], refs[count:]
    latent_ref, query_ref, pair_ref, mixed_ref, peak_ref, sum_ref, score_ref, weight_ref = refs
    nodes, features = query_ref.shape
    sector_rows(
        mean_ref, gain.now(), w_embed, w_encode, w_query, w_key, w_value, feats,
        latent_ref, query_ref, pair_ref,
    )

    def store(at, values, sums, peaks):
        mixed_ref[:, at] = values
        sum_ref[:, at] = sums
        peak_ref[:, at] = peaks

    attention(query_ref, [pair_ref], bias_ref, score_ref, weight_ref, None, store)


def attend_kernel(
    bands, near_ref, *refs
):
    attend_rows([near_ref, *refs[:bands]], *refs[bands:])


def attend_rows(
    pairs, bias_ref, latent_ref, query_ref, mixed_ref, peak_ref, sum_ref,
    w_output, w_decode, gain_dec, w_read, out_ref, score_ref, weight_ref, context_ref,
):
    nodes, features = latent_ref.shape

    def store(at, values, sums, peaks):
        fade = jnp.exp(peak_ref[:, at] - peaks)
        values = values + fade * mixed_ref[:, at]
        context_ref[:, at] = (values / (sums + fade * sum_ref[:, at])).astype(BF16)

    attention(query_ref, pairs, bias_ref, score_ref, weight_ref, peak_ref, store)
    mixed = latent_ref[...] + jnp.dot(context_ref[...], w_output[...], preferred_element_type=F32)
    normed_out = layer_norm(mixed, gain_dec.now()[...]).astype(BF16)
    decoded = silu(jnp.dot(normed_out, w_decode[...], preferred_element_type=F32)).astype(BF16)
    out_ref[...] = lax.dot_general(
        w_read.now()[...], decoded, (((1,), (1,)), ((), ())), preferred_element_type=F32
    ).astype(BF16)


def cell_counts(block, member, part, row, nodes):
    lanes = 2 * block.shape[2]
    iota = lax.broadcasted_iota(jnp.int32, (nodes, lanes), 0).astype(F32).astype(BF16)
    one, none = jnp.ones((nodes, lanes), BF16), jnp.zeros((nodes, lanes), BF16)
    code = jnp.where(block == part, member, -1.0)
    code = jnp.concatenate([code[:, row], code[:, row + 1]], axis=1).astype(BF16)
    counts = none
    for slot in range(code.shape[0]):
        counts = counts + jnp.where(iota == code[slot : slot + 1], one, none)
    return counts


def decode_kernel(bands, sectors, parts, later, dec, reads, base_ref, out_ref, *refs):
    dec_ref = dec.now()
    rows, cols = dec_ref.shape[1:]
    nodes = parts[0][1].stop - parts[0][1].start
    block, member = place_of(dec_ref[...], nodes, bands, sectors)
    for row in range(0, rows, 2):
        at = slice(row * cols, (row + 2) * cols)
        update = None
        for (part, there), read_ref in zip(parts, reads):
            counts = cell_counts(block, member, part, row, nodes)
            share = jnp.dot(read_ref[:, there], counts, preferred_element_type=F32)
            update = share if update is None else update + share
        out_ref[:, at] = base_ref[:, at].astype(F32) + update / 3.0
        for index, part in enumerate(later):
            refs[0][index * nodes : (index + 1) * nodes, at] = cell_counts(
                block, member, part, row, nodes
            )


def finish_kernel(base_ref, read_ref, counts_ref, out_ref, wide, signals):
    rows, cols = wide.shape[1:]
    copies, half = [], rows // 2
    for row in range(0, rows, 2):
        at = slice(row * cols, (row + 2) * cols)
        update = jnp.dot(read_ref[...], counts_ref[:, at], preferred_element_type=F32)
        update = base_ref[:, at] + update / 3.0
        wide[:, row, :] = update[:, :cols]
        wide[:, row + 1, :] = update[:, cols:]
        if (row + 2) % half == 0:
            done = slice(row + 2 - half, row + 2)
            copies.append(
                pltpu.make_async_copy(
                    wide.at[:, done], out_ref.at[:, done], signals.at[len(copies)]
                )
            )
            copies[-1].start()
    for copy in copies:
        copy.wait()


class Late:
    def __init__(self, source, target, semaphore):
        self.target = target
        self.copy = pltpu.make_async_copy(source, target, semaphore)
        self.copy.start()
        self.waited = False

    def now(self):
        if not self.waited:
            self.copy.wait()
            self.waited = True
        return self.target


def call(name, kernel, outs, operands, late=(), scratch=(), mib=8, micros=1, out_memory=pltpu.VMEM):
    single = not isinstance(outs, (list, tuple))
    outs = [outs] if single else list(outs)
    n_in, n_late, n_out = len(operands), len(late), len(outs)

    def run(*refs):
        ins, refs = refs[:n_in], refs[n_in:]
        sources, refs = refs[:n_late], refs[n_late:]
        results, refs = refs[:n_out], refs[n_out:]
        targets, refs = refs[:n_late], refs[n_late:]
        if n_late:
            semaphores, refs = refs[0], refs[1:]
        fetched = [
            Late(source, target, semaphores.at[index])
            for index, (source, target) in enumerate(zip(sources, targets))
        ]
        kernel(*ins, *fetched, *results, *refs)

    fetch = [pltpu.VMEM(a.shape, a.dtype) for a in late]
    signals = [pltpu.SemaphoreType.DMA((n_late,))] if n_late else []
    specs = [whole()] * n_in + [whole(pltpu.HBM)] * n_late
    result = pl.pallas_call(
        run,
        name=name,
        out_shape=outs,
        in_specs=specs,
        out_specs=[whole(out_memory)] * n_out,
        scratch_shapes=fetch + signals + list(scratch),
        compiler_params=params(mib),
        cost_estimate=pl.CostEstimate(
            flops=int(micros * 5e8), bytes_accessed=int(micros * 3e6), transcendentals=0
        ),
    )(*operands, *late)
    return result[0] if single else result


def after(value, *earlier):
    return lax.optimization_barrier((value,) + earlier)[0]


def body(
    grid_state, mesh_feat, enc_src, enc_count, nbr_ids, nbr_count, dec_src,
    w_embed, w_encode, w_query, w_key, w_value, w_output, w_decode, w_readout, norm_attn, norm_dec,
):
    shape = jax.ShapeDtypeStruct
    bands, sectors = lax.axis_size("lat"), lax.axis_size("lon")
    variables, rows, cols = grid_state.shape
    nodes, features = mesh_feat.shape
    slots = enc_src.shape[0]
    cells, rim = rows * cols, rows * HALO
    sector_nodes = bands * nodes

    first = call("first", first_kernel, shape((8, LANES), F32), (), micros=20)
    near_rim, far_rim, live = call(
        "prep",
        prep_kernel,
        [
            shape((variables, rim), BF16),
            shape((variables, rim), BF16),
            shape((slots, nodes), jnp.int32),
        ],
        (first, grid_state, enc_src, enc_count[None]),
        scratch=[pltpu.VMEM((variables, rows, cols), F32)],
        micros=2,
    )
    feat = after(mesh_feat, live)
    far_rim = from_far(far_rim)
    near_rim = from_near(near_rim)
    feats = [mesh_feat] + from_bands(mesh_feat)
    lives = [live] + from_bands(live)
    flat = call(
        "flat",
        flat_kernel,
        shape((variables, cells), BF16),
        (after(grid_state, live),),
        scratch=[pltpu.VMEM((variables, rows, cols), F32)],
        micros=0.1,
    )
    encoded = []
    for step, source in enumerate(lives):
        encoded += call(
            "encode",
            encode_kernel,
            [shape((variables, nodes), F32), shape((2 * rim, nodes), BF16)],
                (source, flat),
            micros=0.1 if step else 3,
        )
    feat_far = from_far(feat)
    summed, sent = call(
        "rim",
        rim_kernel,
        [shape((variables, sector_nodes), F32), shape((variables, sector_nodes), BF16)],
        (near_rim, far_rim, *encoded), micros=0.1,
    )
    received = from_bands(sent)
    bias_own, bias_rest = call(
        "bias",
        functools.partial(bias_kernel, bands, sectors),
        [shape((nodes, sector_nodes), F32), shape((nodes, 2 * sector_nodes), F32)],
        (),
        late=(after(nbr_ids, summed), nbr_count[None]),
        micros=30,
    )
    mean = call(
        "mean",
        mean_kernel,
        shape((variables, sector_nodes), BF16),
        (after(summed, bias_own), *received, *lives),
        micros=0.1,
    )
    feats_far = [feat_far] + from_bands(after(feat_far, mean))
    mean_far = from_far(mean)
    latent, query, pair, mixed, peak, total = call(
        "own",
        functools.partial(own_kernel, len(feats)),
        [
            shape((nodes, features), F32),
            shape((nodes, features), BF16),
            shape((sector_nodes, 2 * features), BF16),
        ]
        + [shape((nodes, features), F32)] * 3,
        (mean, bias_own, after(w_embed, feat_far), w_encode, w_query, w_key, w_value),
        late=(norm_attn[None], *feats),
        scratch=[
            pltpu.VMEM((SLOTS, 2 * nodes, sector_nodes), F32),
            pltpu.VMEM((SLOTS, 2 * nodes, sector_nodes), BF16),
        ],
        mib=20,
        micros=10,
    )
    pair_near = from_near(pair)
    pairs_far = []
    for band, source in enumerate(feats_far):
        at = slice(band * nodes, (band + 1) * nodes)
        pairs_far.append(
            call(
                "far",
                functools.partial(far_kernel, at),
                shape((nodes, 2 * features), BF16),
                (mean_far, after(w_embed, pair, *pairs_far), w_encode, w_key, w_value),
                late=(norm_attn[None], source),
                mib=16,
                micros=60 if band else 0.1,
            )
        )
    readout = call(
        "attend",
        functools.partial(attend_kernel, bands),
        shape((variables, nodes), BF16),
        (pair_near, *pairs_far, bias_rest, latent, query, mixed, peak, total, w_output, w_decode),
        late=(norm_dec[None], w_readout.T),
        scratch=[
            pltpu.VMEM((SLOTS, 2 * nodes, 2 * sector_nodes), F32),
            pltpu.VMEM((SLOTS, 2 * nodes, 2 * sector_nodes), BF16),
            pltpu.VMEM((nodes, features), BF16),
        ],
        mib=40,
        micros=12,
    )
    sums = shape((variables, cells), F32)
    decode = functools.partial(decode_kernel, bands, sectors)
    spots = [slice(band * nodes, (band + 1) * nodes) for band in range(bands)]
    own_sums = call(
        "decode_own",
        lambda read, base, dec, out: decode([(0, spots[0])], [], dec, [read], base, out),
        sums,
        (readout, flat),
        late=(dec_src,),
        micros=0.1,
    )
    reads = jnp.concatenate([readout] + from_bands(readout), axis=1)
    reads = after(reads, own_sums)
    read_far = from_far(reads)
    read_near = from_near(reads)
    far_blocks = [2 * bands + band for band in range(bands)]
    near_sums, far_counts = call(
        "decode_near",
        lambda base, own, near, dec, out, counts: decode(
            list(enumerate(spots))[1:] + list(enumerate(spots, bands)),
            far_blocks, dec, [own] * (bands - 1) + [near] * bands, base, out, counts,
        ),
        [sums, shape((sector_nodes, cells), BF16)],
        (own_sums, reads, read_near),
        late=(dec_src,),
        mib=12,
        micros=0.1,
    )
    return call(
        "finish",
        finish_kernel,
        shape(grid_state.shape, F32),
        (near_sums, read_far, far_counts),
        scratch=[pltpu.VMEM(grid_state.shape, F32), pltpu.SemaphoreType.DMA((2,))],
        out_memory=pltpu.HBM,
        micros=0.1,
    )


def solution(mesh):
    in_specs = (
        P(None, "lat", "lon"),
        P(("lat", "lon"), None),
        P(None, ("lat", "lon")),
        P(("lat", "lon")),
        P(None, ("lat", "lon")),
        P(("lat", "lon")),
        P(None, "lat", "lon"),
    ) + (P(),) * 10
    out_specs = P(None, "lat", "lon")
    return jax.shard_map(body, mesh=mesh, in_specs=in_specs, out_specs=out_specs, check_vma=False)
```
